1024 devices in a mesh: ctx: 16 (over x, y_lo, core), section: 64 (over z, y_hi).
Axes of the slice: x: 4, y: 8 (y_hi: 4, y_lo: 2; y = y_hi * 2 + y_lo), z: 16, core: 2. Of those that a mesh axis runs over, the one named last changes fastest.
Arguments:
- query_in: bfloat16 [64, 2, 2048, 1024], P('section', None, 'ctx'), may hold values from -200 to 200
- key_in: bfloat16 [64, 2, 2048, 128], P('section', None, 'ctx'), may hold values from -5 to 5
- value_in: bfloat16 [64, 2, 2048, 128], P('section', None, 'ctx'), may hold values from -24 to 24
- forward_out: bfloat16 [64, 2, 2048, 1024], P('section', None, 'ctx'), may hold values from -6 to 6
- log_sum: float32 [64, 2, 8, 2048], P('section', None, None, 'ctx'), as said below
- grad_out: bfloat16 [64, 2, 2048, 1024], P('section', None, 'ctx'), may hold values from -6 to 6
- block_order: int32 [32], replicated, may hold values from 0 to 31, each once
Outputs:
- grad_query: bfloat16 [64, 2, 2048, 1024], P('section', None, 'ctx')
- grad_key: bfloat16 [64, 2, 2048, 128], P('section', None, 'ctx')
- grad_value: bfloat16 [64, 2, 2048, 128], P('section', None, 'ctx')
The draws below stay inside these ranges and needn't reach their ends.
Inputs may be any that keep to these rules, and one draw needn't show every extreme that they name: For every layer, micro-batch, head and row, log_sum is at least the logarithm of the sum of exp(score) over all key rows of that row's window, masked or not. block_order is a permutation: slot j, rows j * 64 to j * 64 + 63 of the token dimension, holds sequence positions block_order[j] * 64 onward in order.
All inputs are finite; a program needn't handle non-finite values.
Results may differ from the reference program's by a relative error of at most 0.008.
Values may be sent and summed in bfloat16 or wider, within the bound.
No kernel may reach another device: no remote copies, remote signals or barrier semaphores. Data moves between devices by JAX's collectives and lax.ppermute only.
A program may use at most 32 MiB of HBM per device.

```python
import jax
import jax.numpy as jnp
from jax import lax

HEADS = 8
HEAD = 128
TOK_DEV = 128
MICRO = 2
WINDOW = 3
SECTIONS = 64
TOKENS = 2048
HALF = 64
BLOCKS = 32


def pair_item(key, index):
    item_key = jax.random.fold_in(key, index)
    keys_raw = jnp.clip(jax.random.normal(jax.random.fold_in(item_key, 11), (TOKENS, HEAD), jnp.float32), -5.0, 5.0)
    queries = jnp.clip(jax.random.normal(jax.random.fold_in(item_key, 12), (TOKENS, HEADS, HEAD), jnp.float32), -5.0, 5.0)
    return (queries.reshape(TOKENS, HEADS * HEAD), keys_raw, item_key)


def item_list():
    return jnp.arange(SECTIONS * MICRO, dtype=jnp.int32)


def draw_query_in(key, part):
    items = lax.map(lambda index: pair_item(key, index)[0].astype(jnp.bfloat16), item_list())
    return items.reshape(SECTIONS, MICRO, TOKENS, HEADS * HEAD)


def draw_key_in(key, part):
    items = lax.map(lambda index: pair_item(key, index)[1].astype(jnp.bfloat16), item_list())
    return items.reshape(SECTIONS, MICRO, TOKENS, HEAD)


def log_item(key, index):
    queries, keys_raw, item_key = pair_item(key, index)
    shards = TOKENS // TOK_DEV
    query_low = queries.astype(jnp.bfloat16).astype(jnp.float32).reshape(shards, TOK_DEV, HEADS, HEAD)
    key_low = keys_raw.astype(jnp.bfloat16).astype(jnp.float32).reshape(shards, TOK_DEV, HEAD)
    window_keys = jnp.concatenate([jnp.roll(key_low, offset, axis=0) for offset in range(WINDOW)], axis=1)
    scores = jnp.einsum('cqhd,ckd->chqk', query_low, window_keys, precision=lax.Precision.HIGHEST) / jnp.sqrt(jnp.float32(HEAD))
    top = jnp.max(scores, axis=-1)
    total = jnp.sum(jnp.exp(scores - top[..., None]), axis=-1)
    extra = jnp.exp(jax.random.uniform(jax.random.fold_in(item_key, 14), (shards, HEADS, TOK_DEV), jnp.float32, jnp.log(0.1), jnp.log(2.0)))
    log_rows = top + jnp.log(total + extra)
    return jnp.transpose(log_rows, (1, 0, 2)).reshape(HEADS, TOKENS)


def draw_log_sum(key, part):
    items = lax.map(lambda index: log_item(key, index), item_list())
    return items.reshape(SECTIONS, MICRO, HEADS, TOKENS)


def shard_levels(key, dims, cuts, low, largest):
    def one(axis_at, parts):
        heights = jax.random.uniform(jax.random.fold_in(jax.random.fold_in(key, 6), axis_at), (parts,), jnp.float32, low / len(cuts), largest / len(cuts))
        return jnp.repeat(jnp.exp(heights), dims[axis_at] // parts).reshape((-1,) + (1,) * (len(dims) - axis_at - 1))

    factor_of = one(*cuts[0])
    for cut in cuts[1:]:
        factor_of = factor_of * one(*cut)
    return factor_of


def gaussian(key, shape, deviation, reach, split=(), kind=jnp.bfloat16):
    drawn = deviation * jax.random.normal(key, shape, jnp.float32)
    if split:
        drawn = drawn * shard_levels(key, shape, split, -0.22, 0.18)
    return jnp.clip(drawn, -reach, reach).astype(kind)


def setup_inputs(seed: int = 0) -> dict:
    key_of = jax.random.split(jax.random.key(seed), 8)
    query_in = draw_query_in(jax.random.fold_in(key_of[7], 71), 0)
    key_in = draw_key_in(jax.random.fold_in(key_of[7], 71), 0)
    value_in = gaussian(key_of[2], (SECTIONS, MICRO, TOKENS, HEAD), 4.0, 24.0, ((0, 64), (2, 16)))
    forward_out = gaussian(key_of[3], (SECTIONS, MICRO, TOKENS, HEADS * HEAD), 1.0, 6.0, ((0, 64), (2, 16)))
    log_sum = draw_log_sum(jax.random.fold_in(key_of[7], 71), 0)
    grad_out = gaussian(key_of[5], (SECTIONS, MICRO, TOKENS, HEADS * HEAD), 1.0, 6.0, ((0, 64), (2, 16)))
    block_order = jax.random.permutation(key_of[6], BLOCKS).astype(jnp.int32)
    return {"query_in": query_in, "key_in": key_in, "value_in": value_in, "forward_out": forward_out, "log_sum": log_sum, "grad_out": grad_out, "block_order": block_order}


def place_rows(block_order, length, half_rows):
    row_ids = jnp.arange(length, dtype=jnp.int32)
    slot_ids = row_ids // half_rows
    lookup = (slot_ids[:, None] == jnp.arange(block_order.shape[0], dtype=jnp.int32)[None, :]).astype(jnp.int32)
    return lax.optimization_barrier(jnp.sum(lookup * block_order[None, :], axis=1)) * half_rows + row_ids % half_rows

def round_keep(values_in):
    return lax.optimization_barrier(values_in.astype(jnp.bfloat16)).astype(jnp.float32)

def layer_backward(query_rows, key_rows, value_rows, saved_out, saved_log, upstream, places):
    shards = TOKENS // TOK_DEV
    factor = 1.0 / jnp.sqrt(jnp.float32(HEAD))
    query_heads = query_rows.reshape(shards, TOK_DEV, HEADS, HEAD).astype(jnp.float32)
    grad_heads = upstream.reshape(shards, TOK_DEV, HEADS, HEAD).astype(jnp.float32)
    out_heads = saved_out.reshape(shards, TOK_DEV, HEADS, HEAD).astype(jnp.float32)
    row_dot = jnp.transpose(lax.optimization_barrier(jnp.sum(grad_heads * out_heads, axis=-1)), (0, 2, 1))
    log_rows = jnp.transpose(saved_log.reshape(HEADS, shards, TOK_DEV), (1, 0, 2))
    key_float = key_rows.reshape(shards, TOK_DEV, HEAD).astype(jnp.float32)
    value_float = value_rows.reshape(shards, TOK_DEV, HEAD).astype(jnp.float32)
    place_shards = places.reshape(shards, TOK_DEV)
    grad_query = jnp.zeros((shards, TOK_DEV, HEADS, HEAD), jnp.float32)
    grad_key = jnp.zeros((shards, TOK_DEV, HEAD), jnp.float32)
    grad_value = jnp.zeros((shards, TOK_DEV, HEAD), jnp.float32)
    for offset in range(WINDOW):
        key_near = jnp.roll(key_float, offset, axis=0)
        value_near = jnp.roll(value_float, offset, axis=0)
        place_near = jnp.roll(place_shards, offset, axis=0)
        scores = jnp.einsum('cqhd,ckd->chqk', query_heads, key_near) * factor
        visible = place_shards[:, :, None] >= place_near[:, None, :]
        probs = jnp.where(visible[:, None], jnp.exp(scores - log_rows[..., None]), 0.0)
        grad_probs = jnp.einsum('cqhd,ckd->chqk', grad_heads, value_near)
        grad_scores = round_keep(probs * (grad_probs - row_dot[..., None]))
        probs_low = round_keep(probs)
        grad_query = grad_query + jnp.einsum('chqk,ckd->cqhd', grad_scores, key_near) * factor
        key_terms = jnp.einsum('chqk,cqhd->ckd', grad_scores, query_heads) * factor
        value_terms = jnp.einsum('chqk,cqhd->ckd', probs_low, grad_heads)
        grad_key = grad_key + jnp.roll(key_terms, -offset, axis=0)
        grad_value = grad_value + jnp.roll(value_terms, -offset, axis=0)
    return (grad_query.reshape(TOKENS, HEADS * HEAD).astype(jnp.bfloat16), grad_key.reshape(TOKENS, HEAD).astype(jnp.bfloat16), grad_value.reshape(TOKENS, HEAD).astype(jnp.bfloat16))

def reference(query_in, key_in, value_in, forward_out, log_sum, grad_out, block_order):
    places = place_rows(block_order, TOKENS, HALF)

    def run_layer(items):
        return layer_backward(items[0], items[1], items[2], items[3], items[4], items[5], places)
    first = lax.map(run_layer, (query_in[:, 0], key_in[:, 0], value_in[:, 0], forward_out[:, 0], log_sum[:, 0], grad_out[:, 0]))
    passed = jnp.concatenate([first[0][1:], jnp.zeros_like(first[0][:1])], axis=0)
    upstream = (grad_out[:, 1].astype(jnp.float32) + passed.astype(jnp.float32)).astype(jnp.bfloat16)
    second = lax.map(run_layer, (query_in[:, 1], key_in[:, 1], value_in[:, 1], forward_out[:, 1], log_sum[:, 1], upstream))
    grad_query = jnp.stack([first[0], second[0]], axis=1)
    grad_key = jnp.stack([first[1], second[1]], axis=1)
    grad_value = jnp.stack([first[2], second[2]], axis=1)
    return (grad_query, grad_key, grad_value)
```

```python
import functools
import math

import jax
import jax.numpy as jnp
from jax import lax
from jax.experimental import pallas as pl
from jax.experimental.pallas import tpu as pltpu
from jax.sharding import PartitionSpec as P

WINDOW = 3
PAIR = 2
NT = (((1,), (1,)), ((), ()))
NN = (((1,), (0,)), ((), ()))


def dot(a, b, dims):
    return lax.dot_general(a, b, dims, preferred_element_type=jnp.float32)


def ring(value, steps):
    count = lax.axis_size("ctx")
    return lax.ppermute(value, "ctx", [(i, (i + steps) % count) for i in range(count)])


def down(value):
    count = lax.axis_size("section")
    return lax.ppermute(value, "section", [(i, i - 1) for i in range(1, count)])


def mask_bias(order_ref, rows):
    half = rows // 2
    slots = order_ref.shape[0]
    own = lax.axis_index("ctx")
    lane = lax.broadcasted_iota(jnp.int32, (half, rows), 1)
    sub = lax.broadcasted_iota(jnp.int32, (half, rows), 0)
    query = jnp.where(
        lane < half,
        order_ref[2 * own] * half + lane,
        order_ref[2 * own + 1] * half + lane - half,
    )
    blocks = []
    for offset in range(WINDOW):
        for part in range(2):
            slot = lax.rem(2 * (own - offset) + part + slots, slots)
            blocks.append(jnp.where(order_ref[slot] * half + sub <= query, 0.0, -1e30))
    return jnp.concatenate(blocks, axis=0)


def stacked(block, first, size):
    return jnp.concatenate(
        [block[:, (first + i) * size : (first + i + 1) * size] for i in range(PAIR)], axis=0
    )


def head_rows(table, first):
    return jnp.concatenate([table[first + i : first + i + 1] for i in range(PAIR)], axis=1)


def dots_of_rows(upstream, out, heads, size):
    product = upstream.astype(jnp.float32) * out.astype(jnp.float32)
    high = product.astype(jnp.bfloat16)
    low = (product - high.astype(jnp.float32)).astype(jnp.bfloat16)
    pick = (
        lax.broadcasted_iota(jnp.int32, (heads, heads * size), 1) // size
        == lax.broadcasted_iota(jnp.int32, (heads, heads * size), 0)
    ).astype(jnp.float32).astype(jnp.bfloat16)
    return dot(pick, high, NT) + dot(pick, low, NT)


def window_of(refs, which):
    return jnp.concatenate([ref[0, which] for ref in refs], axis=0)


def scores_back(query, grad, keys, values, bias, log_row, dot_row, factor):
    scores = dot(keys, query, NT)
    probs = jnp.exp(scores * factor + (bias - log_row))
    grad_probs = dot(values, grad, NT)
    return probs.astype(jnp.bfloat16), (probs * (grad_probs - dot_row)).astype(jnp.bfloat16)


def query_kernel(factor, order_ref, q_ref, g_ref, o_ref, log_ref, kv0, kv1, kv2, dq_ref):
    query, grad, log_rows = q_ref[0, 0], g_ref[0, 0], log_ref[0, 0]
    rows, size = query.shape[0], kv0.shape[3]
    heads = query.shape[1] // size
    keys, values = window_of((kv0, kv1, kv2), 0), window_of((kv0, kv1, kv2), 1)
    keys_t = keys.T
    bias = mask_bias(order_ref, rows)
    bias = jnp.concatenate([bias] * PAIR, axis=1)
    dot_rows = dots_of_rows(grad, o_ref[0, 0], heads, size)
    for first in range(0, heads, PAIR):
        _, grad_scores = scores_back(
            stacked(query, first, size),
            stacked(grad, first, size),
            keys,
            values,
            bias,
            head_rows(log_rows, first),
            head_rows(dot_rows, first),
            factor,
        )
        part = (dot(keys_t, grad_scores, NN) * factor).T.astype(jnp.bfloat16)
        for i in range(PAIR):
            dq_ref[:, (first + i) * size : (first + i + 1) * size] = part[i * rows : (i + 1) * rows]


def pair_kernel(factor, micro, order_ref, q_ref, g_ref, o_ref, log_ref, kv0, kv1, kv2, *refs):
    if micro:
        r_ref, _, gq_ref, own_ref, near_ref, far_ref = refs
    else:
        dq_ref, gq_ref, own_ref, near_ref, far_ref = refs
    query, grad, log_rows = q_ref[0, 0], g_ref[0, 0], log_ref[0, 0]
    if micro:
        grad = (grad.astype(jnp.float32) + r_ref[...].astype(jnp.float32)).astype(jnp.bfloat16)
    else:
        gq_ref[0, 0] = dq_ref[...]
    rows, size = query.shape[0], kv0.shape[3]
    heads = query.shape[1] // size
    keys, values = window_of((kv0, kv1, kv2), 0), window_of((kv0, kv1, kv2), 1)
    keys_t = keys.T
    bias = mask_bias(order_ref, rows)
    bias = jnp.concatenate([bias] * PAIR, axis=1)
    dot_rows = dots_of_rows(grad, o_ref[0, 0], heads, size)
    key_sum = value_sum = None
    for first in range(0, heads, PAIR):
        query_pair, grad_pair = stacked(query, first, size), stacked(grad, first, size)
        probs, grad_scores = scores_back(
            query_pair,
            grad_pair,
            keys,
            values,
            bias,
            head_rows(log_rows, first),
            head_rows(dot_rows, first),
            factor,
        )
        key_part = dot(grad_scores, query_pair, NN)
        value_part = dot(probs, grad_pair, NN)
        key_sum = key_part if key_sum is None else key_sum + key_part
        value_sum = value_part if value_sum is None else value_sum + value_part
        if micro:
            part = (dot(keys_t, grad_scores, NN) * factor).T.astype(jnp.bfloat16)
            for i in range(PAIR):
                gq_ref[0, 0, :, (first + i) * size : (first + i + 1) * size] = part[
                    i * rows : (i + 1) * rows
                ]
    key_sum = key_sum * factor
    own_ref[0], own_ref[1] = key_sum[:rows], value_sum[:rows]
    for offset, ref in ((1, near_ref), (2, far_ref)):
        ref[0] = key_sum[offset * rows : (offset + 1) * rows].astype(jnp.bfloat16)
        ref[1] = value_sum[offset * rows : (offset + 1) * rows].astype(jnp.bfloat16)


def sum_kernel(own0, near0, far0, own1, near1, far1, gk_ref, gv_ref):
    for micro, (own, near, far) in enumerate(((own0, near0, far0), (own1, near1, far1))):
        for which, ref in ((0, gk_ref), (1, gv_ref)):
            total = own[which] + near[which].astype(jnp.float32) + far[which].astype(jnp.float32)
            ref[0, micro] = total.astype(jnp.bfloat16)


def cost(rows, heads, size, products):
    flops = 2 * rows * heads * WINDOW * rows * size * products
    return pl.CostEstimate(
        flops=flops, bytes_accessed=4 * rows * heads * size * 2, transcendentals=rows * heads * WINDOW * rows
    )


def shards(query_in, key_in, value_in, forward_out, log_sum, grad_out, block_order):
    rows, width = query_in.shape[2:]
    size = key_in.shape[3]
    heads = width // size
    factor = 1.0 / math.sqrt(size)
    params = pltpu.CompilerParams(vmem_limit_bytes=48 * 2**20)

    def whole(shape):
        return pl.BlockSpec(shape, lambda i: (0,) * len(shape))

    def at(shape, micro):
        return pl.BlockSpec(shape, lambda i: (0, micro) + (0,) * (len(shape) - 2))

    def pair_at(micro):
        return pl.BlockSpec((1, 2, rows, size), lambda i: (micro, 0, 0, 0))

    def in_specs(micro):
        return [
            pl.BlockSpec(memory_space=pltpu.SMEM),
            at((1, 1, rows, width), micro),
            at((1, 1, rows, width), micro),
            at((1, 1, rows, width), micro),
            at((1, 1, heads, rows), micro),
        ] + [pair_at(micro)] * WINDOW

    key_value = jnp.stack([key_in[0], value_in[0]], axis=1)
    window = (key_value, ring(key_value, 1), ring(key_value, 2))
    common = (block_order, query_in, grad_out, forward_out, log_sum, *window)

    dq = pl.pallas_call(
        functools.partial(query_kernel, factor),
        grid=(1,),
        in_specs=in_specs(0),
        out_specs=whole((rows, width)),
        out_shape=jax.ShapeDtypeStruct((rows, width), jnp.bfloat16),
        compiler_params=params,
        cost_estimate=cost(rows, heads, size, 3),
        name="query_first",
    )(*common)
    received = down(dq)

    terms_shape = [
        jax.ShapeDtypeStruct((1, 2, rows, width), jnp.bfloat16),
        jax.ShapeDtypeStruct((2, rows, size), jnp.float32),
        jax.ShapeDtypeStruct((2, rows, size), jnp.bfloat16),
        jax.ShapeDtypeStruct((2, rows, size), jnp.bfloat16),
    ]
    term_specs = [whole((2, rows, size))] * 3
    grad_query, own0, near0, far0 = pl.pallas_call(
        functools.partial(pair_kernel, factor, 0),
        grid=(1,),
        in_specs=in_specs(0) + [whole((rows, width))],
        out_specs=[at((1, 1, rows, width), 0)] + term_specs,
        out_shape=terms_shape,
        compiler_params=params,
        cost_estimate=cost(rows, heads, size, 4),
        name="pairs_first",
    )(*common, dq)
    far0, near0 = ring(far0, -2), ring(near0, -1)

    grad_query, own1, near1, far1 = pl.pallas_call(
        functools.partial(pair_kernel, factor, 1),
        grid=(1,),
        in_specs=in_specs(1) + [whole((rows, width)), pl.BlockSpec(memory_space=pl.ANY)],
        out_specs=[at((1, 1, rows, width), 1)] + term_specs,
        out_shape=terms_shape,
        input_output_aliases={9: 0},
        compiler_params=params,
        cost_estimate=cost(rows, heads, size, 5),
        name="pairs_second",
    )(*common, received, grad_query)
    far1, near1 = ring(far1, -2), ring(near1, -1)

    grad_key, grad_value = pl.pallas_call(
        sum_kernel,
        out_shape=[jax.ShapeDtypeStruct((1, 2, rows, size), jnp.bfloat16)] * 2,
        compiler_params=params,
        name="sums",
    )(own0, near0, far0, own1, near1, far1)
    return (grad_query, grad_key, grad_value)


def solution(mesh):
    split = P("section", None, "ctx", None)
    return jax.shard_map(
        shards,
        mesh=mesh,
        in_specs=(split, split, split, split, P("section", None, None, "ctx"), split, P()),
        out_specs=(split, split, split),
        check_vma=False,
    )
```

```python
import functools
import math

import jax
import jax.numpy as jnp
from jax import lax
from jax.experimental import pallas as pl
from jax.experimental.pallas import tpu as pltpu
from jax.sharding import PartitionSpec as P

WINDOW = 3
PAIR = 2
NT = (((1,), (1,)), ((), ()))
NN = (((1,), (0,)), ((), ()))
LOW = jnp.bfloat16
WIDE = jnp.float32


def dot(a, b, dims=NN):
    return lax.dot_general(a, b, dims, preferred_element_type=WIDE)


def ring(value, steps):
    count = lax.axis_size("ctx")
    return lax.ppermute(value, "ctx", [(i, (i + steps) % count) for i in range(count)])


def down(value):
    count = lax.axis_size("section")
    return lax.ppermute(value, "section", [(i, i - 1) for i in range(1, count)])


def mask_bias(order_ref, rows, offsets):
    half = rows // 2
    slots = order_ref.shape[0]
    own = lax.axis_index("ctx")
    lane = lax.broadcasted_iota(jnp.int32, (half, rows), 1)
    sub = lax.broadcasted_iota(jnp.int32, (half, rows), 0)
    query = jnp.where(
        lane < half,
        order_ref[2 * own] * half + lane,
        order_ref[2 * own + 1] * half + lane - half,
    )
    blocks = []
    for offset in offsets:
        for part in range(2):
            slot = lax.rem(2 * (own - offset) + part + slots, slots)
            blocks.append(jnp.where(order_ref[slot] * half + sub <= query, 0.0, -1e30))
    bias = jnp.concatenate(blocks, axis=0)
    return jnp.concatenate([bias] * PAIR, axis=1)


def stacked(block, size):
    return jnp.concatenate(
        [block[:, i * size : (i + 1) * size] for i in range(block.shape[1] // size)], axis=0
    )


def head_rows(table, first):
    return jnp.concatenate([table[first + i : first + i + 1] for i in range(PAIR)], axis=1)


def dots_of_rows(upstream, out, size):
    product = upstream.astype(WIDE) * out.astype(WIDE)
    high = product.astype(LOW)
    low = (product - high.astype(WIDE)).astype(LOW)
    shape = (8, product.shape[1])
    pick = (lax.broadcasted_iota(jnp.int32, shape, 1) // size == lax.broadcasted_iota(jnp.int32, shape, 0)).astype(WIDE).astype(LOW)
    return dot(pick, high, NT) + dot(pick, low, NT)


def turned(part, rows):
    count = part.shape[1] // rows
    return jnp.concatenate([part[:, i * rows : (i + 1) * rows].T for i in range(count)], axis=1)


def joined(refs, micro, which):
    return jnp.concatenate([ref[micro, which] for ref in refs], axis=0)


def own_kernel(factor, order_ref, log_ref, kv_ref, q_hbm, g_hbm, o_hbm, qs_ref, gs_ref, rd_ref, dqt_ref, own_ref, q_v, g_v, o_v, sems):
    copies = [
        pltpu.make_async_copy(source.at[0, 0], target, sems.at[i])
        for i, (source, target) in enumerate(((g_hbm, g_v), (o_hbm, o_v), (q_hbm, q_v)))
    ]
    for copy in copies:
        copy.start()
    rows, size = kv_ref.shape[2], kv_ref.shape[3]
    keys, values = kv_ref[0, 0], kv_ref[0, 1]
    keys_t = keys.T
    bias = mask_bias(order_ref, rows, (0,))
    log_rows = log_ref[0, 0]
    copies[0].wait()
    copies[1].wait()
    grad = stacked(g_v[...], size)
    gs_ref[...] = grad
    dot_rows = dots_of_rows(g_v[...], o_v[...], size)
    rd_ref[...] = dot_rows
    copies[2].wait()
    query = stacked(q_v[...], size)
    qs_ref[...] = query
    step = PAIR * rows
    key_sum = value_sum = 0.0
    for first in range(0, query.shape[0] // rows, PAIR):
        cut = slice(first * rows, first * rows + step)
        probs = jnp.exp(dot(keys, query[cut], NT) * factor + (bias - head_rows(log_rows, first)))
        grad_scores = (probs * (dot(values, grad[cut], NT) - head_rows(dot_rows, first))).astype(LOW)
        dqt_ref[:, cut] = dot(keys_t, grad_scores)
        key_sum += dot(grad_scores, query[cut])
        value_sum += dot(probs.astype(LOW), grad[cut])
    own_ref[0] = key_sum * factor
    own_ref[1] = value_sum


def query_kernel(factor, start, order_ref, log_ref, kv1, kv2, qs_ref, gs_ref, rd_ref, dqt_ref, dq_ref):
    rows, size = kv1.shape[2], kv1.shape[3]
    keys, values = joined((kv1, kv2), 0, 0), joined((kv1, kv2), 0, 1)
    keys_t = keys.T
    bias = mask_bias(order_ref, rows, (1, 2))
    log_rows, dot_rows = log_ref[0, 0], rd_ref[...]
    step = PAIR * rows
    for first in range(start, start + dq_ref.shape[1] // size, PAIR):
        cut = slice(first * rows, first * rows + step)
        probs = jnp.exp(dot(keys, qs_ref[cut], NT) * factor + (bias - head_rows(log_rows, first)))
        grad_scores = (probs * (dot(values, gs_ref[cut], NT) - head_rows(dot_rows, first))).astype(LOW)
        part = (dot(keys_t, grad_scores) + dqt_ref[:, cut]) * factor
        at = (first - start) * size
        dq_ref[:, at : at + PAIR * size] = turned(part, rows).astype(LOW)


def middle_kernel(
    factor, order_ref, log_ref, kv0, kv1, kv2, qs_ref, gs_ref, rd_ref, dqa_ref, dqb_ref, q_hbm, g_hbm, o_hbm,
    gq_hbm, near_ref, far_ref, qs1_ref, g1_ref, o1_ref, probs_ref, q_v, sems,
):
    half = dqa_ref.shape[1]
    copies = [
        pltpu.make_async_copy(q_hbm.at[0, 1], q_v, sems.at[0]),
        pltpu.make_async_copy(g_hbm.at[0, 1], g1_ref, sems.at[1]),
        pltpu.make_async_copy(o_hbm.at[0, 1], o1_ref, sems.at[2]),
        pltpu.make_async_copy(dqa_ref, gq_hbm.at[0, 0, :, pl.ds(0, half)], sems.at[3]),
        pltpu.make_async_copy(dqb_ref, gq_hbm.at[0, 0, :, pl.ds(half, half)], sems.at[4]),
    ]
    for copy in copies:
        copy.start()
    rows, size = kv1.shape[2], kv1.shape[3]
    heads = qs_ref.shape[0] // rows
    keys, values = joined((kv1, kv2), 0, 0), joined((kv1, kv2), 0, 1)
    bias = mask_bias(order_ref, rows, (0, 1, 2))
    log_rows, dot_rows = log_ref[0, 0], rd_ref[...]
    step = PAIR * rows
    key_sum = value_sum = 0.0
    for first in range(0, heads, PAIR):
        cut = slice(first * rows, first * rows + step)
        query, grad = qs_ref[cut], gs_ref[cut]
        probs = jnp.exp(dot(keys, query, NT) * factor + (bias[rows:] - head_rows(log_rows, first)))
        grad_scores = (probs * (dot(values, grad, NT) - head_rows(dot_rows, first))).astype(LOW)
        key_sum += dot(grad_scores, query)
        value_sum += dot(probs.astype(LOW), grad)
    key_sum = key_sum * factor
    for i, ref in enumerate((near_ref, far_ref)):
        ref[0] = key_sum[i * rows : (i + 1) * rows].astype(LOW)
        ref[1] = value_sum[i * rows : (i + 1) * rows].astype(LOW)
    copies[0].wait()
    query = stacked(q_v[...], size)
    qs1_ref[...] = query
    keys = joined((kv0, kv1, kv2), 1, 0)
    log_rows = log_ref[0, 1]
    for first in range(0, heads, PAIR):
        cut = slice(first * rows, first * rows + step)
        scores = dot(keys, query[cut], NT)
        probs_ref[:, cut] = jnp.exp(scores * factor + (bias - head_rows(log_rows, first)))
    for copy in copies[1:]:
        copy.wait()


def second_kernel(factor, kv0, kv1, kv2, qs_ref, g_ref, o_ref, probs_ref, r_ref, dq_ref, sum_ref):
    rows, size = kv1.shape[2], kv1.shape[3]
    keys, values = joined((kv0, kv1, kv2), 1, 0), joined((kv0, kv1, kv2), 1, 1)
    keys_t = keys.T
    width = r_ref.shape[1]
    upstream = (g_ref[:, :width].astype(WIDE) + r_ref[...].astype(WIDE)).astype(LOW)
    dot_rows = dots_of_rows(upstream, o_ref[:, :width], size)
    upstream = stacked(upstream, size)
    step = PAIR * rows
    key_sum = value_sum = 0.0
    for first in range(0, width // size, PAIR):
        cut = slice(first * rows, first * rows + step)
        probs, grad = probs_ref[:, cut], upstream[cut]
        grad_scores = (probs * (dot(values, grad, NT) - head_rows(dot_rows, first))).astype(LOW)
        key_sum += dot(grad_scores, qs_ref[cut])
        value_sum += dot(probs.astype(LOW), grad)
        part = dot(keys_t, grad_scores) * factor
        dq_ref[:, first * size : (first + PAIR) * size] = turned(part, rows).astype(LOW)
    sum_ref[0] = key_sum
    sum_ref[1] = value_sum


def third_kernel(factor, kv0, kv1, kv2, qs_ref, g_ref, o_ref, probs_ref, sum_ref, r_ref, near_ref, far_ref, up_ref, gs_ref):
    rows, size = kv1.shape[2], kv1.shape[3]
    values = joined((kv0, kv1, kv2), 1, 1)
    width = r_ref.shape[1]
    upstream = (g_ref[:, width:].astype(WIDE) + r_ref[...].astype(WIDE)).astype(LOW)
    dot_rows = dots_of_rows(upstream, o_ref[:, width:], size)
    upstream = stacked(upstream, size)
    up_ref[...] = upstream
    step = PAIR * rows
    base = width // size * rows
    key_sum, value_sum = sum_ref[0, rows:], sum_ref[1, rows:]
    for first in range(0, width // size, PAIR):
        cut = slice(first * rows, first * rows + step)
        far = slice(base + first * rows, base + first * rows + step)
        probs, grad = probs_ref[:, far], upstream[cut]
        grad_scores = (probs * (dot(values, grad, NT) - head_rows(dot_rows, first))).astype(LOW)
        gs_ref[:, cut] = grad_scores
        key_sum += dot(grad_scores[rows:], qs_ref[far])
        value_sum += dot(probs[rows:].astype(LOW), grad)
    key_sum = key_sum * factor
    for i, ref in enumerate((near_ref, far_ref)):
        ref[0] = key_sum[i * rows : (i + 1) * rows].astype(LOW)
        ref[1] = value_sum[i * rows : (i + 1) * rows].astype(LOW)


def fourth_kernel(factor, kv0, kv1, kv2, qs_ref, probs_ref, sum_ref, up_ref, gs_ref, dqa_ref, _, own_ref, gq_hbm, dqb_v, sems):
    rows = kv1.shape[2]
    half = dqa_ref.shape[1]
    first_copy = pltpu.make_async_copy(dqa_ref, gq_hbm.at[0, 1, :, pl.ds(0, half)], sems.at[0])
    first_copy.start()
    keys_t = joined((kv0, kv1, kv2), 1, 0).T
    base = up_ref.shape[0]
    dqb_v[...] = turned(dot(keys_t, gs_ref[...]) * factor, rows).astype(LOW)
    last_copy = pltpu.make_async_copy(dqb_v, gq_hbm.at[0, 1, :, pl.ds(half, half)], sems.at[1])
    last_copy.start()
    own_ref[0] = (sum_ref[0, :rows] + dot(gs_ref[:rows], qs_ref[base:])) * factor
    own_ref[1] = sum_ref[1, :rows] + dot(probs_ref[:rows, base:].astype(LOW), up_ref[...])
    first_copy.wait()
    last_copy.wait()


def sum_kernel(own0, near0, far0, own1, near1, far1, gk_ref, gv_ref):
    for micro, (own, near, far) in enumerate(((own0, near0, far0), (own1, near1, far1))):
        for which, ref in ((0, gk_ref), (1, gv_ref)):
            total = own[which] + near[which].astype(WIDE) + far[which].astype(WIDE)
            ref[0, micro] = total.astype(LOW)


VM = pl.BlockSpec(memory_space=pltpu.VMEM)
SM = pl.BlockSpec(memory_space=pltpu.SMEM)
HB = pl.BlockSpec(memory_space=pltpu.HBM)


def shards(query_in, key_in, value_in, forward_out, log_sum, grad_out, block_order):
    rows, width = query_in.shape[2:]
    size = key_in.shape[3]
    heads = width // size
    half = width // 2
    near_rows = WINDOW * rows
    factor = 1.0 / math.sqrt(size)

    def low(*shape):
        return jax.ShapeDtypeStruct(shape, LOW)

    def wide(*shape):
        return jax.ShapeDtypeStruct(shape, WIDE)

    def call(body, name, ins, outs, in_specs=None, out_specs=None, scratch=(), share=1.0, **more):
        flops = int(2 * near_rows * heads * rows * size * share)
        return pl.pallas_call(
            body,
            in_specs=in_specs or [VM] * len(ins),
            out_specs=out_specs or [VM] * len(outs),
            out_shape=outs,
            scratch_shapes=list(scratch),
            compiler_params=pltpu.CompilerParams(vmem_limit_bytes=40 * 2**20),
            cost_estimate=pl.CostEstimate(flops=flops, bytes_accessed=2**20, transcendentals=near_rows * heads * rows),
            name=name,
            **more,
        )(*ins)

    dma = pltpu.SemaphoreType.DMA
    kv0 = jnp.stack([key_in[0], value_in[0]], axis=1)
    kv2, kv1 = ring(kv0, 2), ring(kv0, 1)
    pair = (2, rows, size)

    qs, gs, rd, dqt, own0 = call(
        functools.partial(own_kernel, factor),
        "own_terms",
        (block_order, log_sum, kv0, query_in, grad_out, forward_out),
        [low(heads * rows, size), low(heads * rows, size), wide(8, rows), wide(size, heads * rows), wide(*pair)],
        in_specs=[SM, VM, VM, HB, HB, HB],
        scratch=[pltpu.VMEM((rows, width), LOW)] * 3 + [dma((3,))],
        share=2,
    )
    parts, received = [], []
    for start in (0, heads // 2):
        (part,) = call(
            functools.partial(query_kernel, factor, start),
            "query_part",
            (block_order, log_sum, kv1, kv2, qs, gs, rd, dqt),
            [low(rows, half)],
            in_specs=[SM] + [VM] * 7,
        )
        parts.append(part)
        received.append(down(part))

    grad_query, near0, far0, qs1, g1, o1, probs = call(
        functools.partial(middle_kernel, factor),
        "middle_terms",
        (block_order, log_sum, kv0, kv1, kv2, qs, gs, rd, *parts, query_in, grad_out, forward_out),
        [low(*query_in.shape), low(*pair), low(*pair), low(heads * rows, size), low(rows, width), low(rows, width), wide(near_rows, heads * rows)],
        in_specs=[SM] + [VM] * 9 + [HB] * 3,
        out_specs=[HB] + [VM] * 6,
        scratch=[pltpu.VMEM((rows, width), LOW), dma((5,))],
        share=4,
    )
    far0, near0 = ring(far0, -2), ring(near0, -1)

    dqa, sums = call(
        functools.partial(second_kernel, factor),
        "second_all",
        (kv0, kv1, kv2, qs1, g1, o1, probs, received[0]),
        [low(rows, half), wide(2, near_rows, size)],
        share=2,
    )
    near1, far1, up, grad_scores = call(
        functools.partial(third_kernel, factor),
        "second_far",
        (kv0, kv1, kv2, qs1, g1, o1, probs, sums, received[1]),
        [low(*pair), low(*pair), low(heads // 2 * rows, size), low(near_rows, heads // 2 * rows)],
    )
    far1, near1 = ring(far1, -2), ring(near1, -1)
    own1, grad_query = call(
        functools.partial(fourth_kernel, factor),
        "second_own",
        (kv0, kv1, kv2, qs1, probs, sums, up, grad_scores, dqa, grad_query),
        [wide(*pair), low(*query_in.shape)],
        in_specs=[VM] * 9 + [HB],
        out_specs=[VM, HB],
        scratch=[pltpu.VMEM((rows, half), LOW), dma((2,))],
        input_output_aliases={9: 1},
    )
    grad_key, grad_value = call(
        sum_kernel,
        "sums",
        (own0, near0, far0, own1, near1, far1),
        [low(1, 2, rows, size)] * 2,
        share=0.01,
    )
    return (grad_query, grad_key, grad_value)


def solution(mesh):
    split = P("section", None, "ctx", None)
    return jax.shard_map(
        shards,
        mesh=mesh,
        in_specs=(split, split, split, split, P("section", None, None, "ctx"), split, P()),
        out_specs=(split, split, split),
        check_vma=False,
    )
```

```python
import functools
import math

import jax
import jax.numpy as jnp
from jax import lax
from jax.experimental import pallas as pl
from jax.experimental.pallas import tpu as pltpu
from jax.sharding import PartitionSpec as P

WINDOW = 3
PAIR = 2
NT = (((1,), (1,)), ((), ()))
NN = (((1,), (0,)), ((), ()))
LOW = jnp.bfloat16
WIDE = jnp.float32


def dot(a, b, dims=NN):
    return lax.dot_general(a, b, dims, preferred_element_type=WIDE)


def ring(value, steps, sections=None):
    count = lax.axis_size("ctx")
    if sections is None:
        return lax.ppermute(value, "ctx", [(i, (i + steps) % count) for i in range(count)])
    layers = lax.axis_size("section")
    route = [(i * layers + s, (i + steps) % count * layers + s) for s in sections for i in range(count)]
    return lax.ppermute(value, ("ctx", "section"), route)


def down(value):
    count = lax.axis_size("section")
    return lax.ppermute(value, "section", [(i, i - 1) for i in range(1, count)])


def mask_bias(order_ref, rows, offsets):
    half = rows // 2
    slots = order_ref.shape[0]
    own = lax.axis_index("ctx")
    lane = lax.broadcasted_iota(jnp.int32, (half, rows), 1)
    sub = lax.broadcasted_iota(jnp.int32, (half, rows), 0)
    query = jnp.where(
        lane < half,
        order_ref[2 * own] * half + lane,
        order_ref[2 * own + 1] * half + lane - half,
    )
    blocks = []
    for offset in offsets:
        for part in range(2):
            slot = lax.rem(2 * (own - offset) + part + slots, slots)
            blocks.append(jnp.where(order_ref[slot] * half + sub <= query, 0.0, -1e30))
    return jnp.concatenate(blocks, axis=0)


def wider(bias):
    return jnp.concatenate([bias] * PAIR, axis=1)


def stacked(block, size):
    return jnp.concatenate(
        [block[:, i * size : (i + 1) * size] for i in range(block.shape[1] // size)], axis=0
    )


def head_rows(table, first):
    return jnp.concatenate([table[first + i : first + i + 1] for i in range(PAIR)], axis=1)


def dots_of_rows(upstream, out, size):
    product = upstream.astype(WIDE) * out.astype(WIDE)
    high = product.astype(LOW)
    low = (product - high.astype(WIDE)).astype(LOW)
    shape = (8, product.shape[1])
    pick = (lax.broadcasted_iota(jnp.int32, shape, 1) // size == lax.broadcasted_iota(jnp.int32, shape, 0)).astype(WIDE).astype(LOW)
    return dot(pick, high, NT) + dot(pick, low, NT)


def turned(part, rows):
    count = part.shape[1] // rows
    return jnp.concatenate([part[:, i * rows : (i + 1) * rows].T for i in range(count)], axis=1)


def joined(refs, micro, which):
    return jnp.concatenate([ref[micro, which] for ref in refs], axis=0)


def own_kernel(
    factor, order_hbm, log_hbm, kv_ref, q_hbm, g_hbm, o_hbm,
    qs_ref, gs_ref, rd_ref, dqt_ref, own_ref, bias_ref, log_ref, order_s, q_v, g_v, o_v, sems,
):
    copies = [
        pltpu.make_async_copy(source, target, sems.at[i])
        for i, (source, target) in enumerate(
            (
                (order_hbm, order_s),
                (g_hbm.at[0, 0], g_v),
                (o_hbm.at[0, 0], o_v),
                (q_hbm.at[0, 0], q_v),
                (log_hbm.at[0], log_ref),
            )
        )
    ]
    for copy in copies:
        copy.start()
    rows, size = kv_ref.shape[2], kv_ref.shape[3]
    keys, values = kv_ref[0, 0], kv_ref[0, 1]
    keys_t = keys.T
    copies[0].wait()
    bias = mask_bias(order_s, rows, range(WINDOW))
    bias_ref[...] = bias
    bias = wider(bias[:rows])
    copies[1].wait()
    copies[2].wait()
    grad = stacked(g_v[...], size)
    gs_ref[...] = grad
    dot_rows = dots_of_rows(g_v[...], o_v[...], size)
    rd_ref[...] = dot_rows
    copies[3].wait()
    query = stacked(q_v[...], size)
    qs_ref[...] = query
    copies[4].wait()
    log_rows = log_ref[0]
    step = PAIR * rows
    key_sum = value_sum = 0.0
    for first in range(0, query.shape[0] // rows, PAIR):
        cut = slice(first * rows, first * rows + step)
        probs = jnp.exp(dot(keys, query[cut], NT) * factor + (bias - head_rows(log_rows, first)))
        grad_scores = (probs * (dot(values, grad[cut], NT) - head_rows(dot_rows, first))).astype(LOW)
        dqt_ref[:, cut] = dot(keys_t, grad_scores)
        key_sum += dot(grad_scores, query[cut])
        value_sum += dot(probs.astype(LOW), grad[cut])
    own_ref[0] = key_sum * factor
    own_ref[1] = value_sum


def query_kernel(factor, bias_ref, log_ref, kv1, kv2, qs_ref, gs_ref, rd_ref, dqt_ref, dq_ref):
    rows, size = kv1.shape[2], kv1.shape[3]
    keys, values = joined((kv1, kv2), 0, 0), joined((kv1, kv2), 0, 1)
    keys_t = keys.T
    bias = wider(bias_ref[rows:])
    log_rows, dot_rows = log_ref[0], rd_ref[...]
    step = PAIR * rows
    for first in range(0, dq_ref.shape[1] // size, PAIR):
        cut = slice(first * rows, first * rows + step)
        probs = jnp.exp(dot(keys, qs_ref[cut], NT) * factor + (bias - head_rows(log_rows, first)))
        grad_scores = (probs * (dot(values, gs_ref[cut], NT) - head_rows(dot_rows, first))).astype(LOW)
        part = (dot(keys_t, grad_scores) + dqt_ref[:, cut]) * factor
        dq_ref[:, first * size : (first + PAIR) * size] = turned(part, rows).astype(LOW)


def middle_kernel(
    factor, bias_ref, log_ref, kv0, kv1, kv2, kv1_first, kv2_first, qs_ref, gs_ref, rd_ref, dqt_ref, q_hbm, g_hbm, o_hbm,
    gq_hbm, near_ref, far_ref, qs1_ref, g1_ref, o1_ref, probs_ref, win_ref, q_v, dq_v, sems,
):
    copies = [
        pltpu.make_async_copy(q_hbm.at[0, 1], q_v, sems.at[0]),
        pltpu.make_async_copy(g_hbm.at[0, 1], g1_ref, sems.at[1]),
        pltpu.make_async_copy(o_hbm.at[0, 1], o1_ref, sems.at[2]),
    ]
    for copy in copies:
        copy.start()
    rows, size = kv1.shape[2], kv1.shape[3]
    heads = qs_ref.shape[0] // rows
    bottom = lax.axis_index("section") == 0

    def window(micro, which):
        near = jnp.where(bottom, kv1_first[micro, which], kv1[micro, which])
        far = jnp.where(bottom, kv2_first[micro, which], kv2[micro, which])
        return jnp.concatenate([near, far], axis=0)

    keys, values = window(0, 0), window(0, 1)
    keys_t = keys.T
    bias = wider(bias_ref[...])
    log_rows, dot_rows = log_ref[0], rd_ref[...]
    step = PAIR * rows
    key_sum = value_sum = 0.0
    for first in range(0, heads, PAIR):
        cut = slice(first * rows, first * rows + step)
        query, grad = qs_ref[cut], gs_ref[cut]
        probs = jnp.exp(dot(keys, query, NT) * factor + (bias[rows:] - head_rows(log_rows, first)))
        grad_scores = (probs * (dot(values, grad, NT) - head_rows(dot_rows, first))).astype(LOW)
        key_sum += dot(grad_scores, query)
        value_sum += dot(probs.astype(LOW), grad)
        part = (dot(keys_t, grad_scores) + dqt_ref[:, cut]) * factor
        dq_v[:, first * size : (first + PAIR) * size] = turned(part, rows).astype(LOW)
    back = pltpu.make_async_copy(dq_v, gq_hbm.at[0, 0], sems.at[3])
    back.start()
    key_sum = key_sum * factor
    for i, ref in enumerate((near_ref, far_ref)):
        ref[0] = key_sum[i * rows : (i + 1) * rows].astype(LOW)
        ref[1] = value_sum[i * rows : (i + 1) * rows].astype(LOW)
    copies[0].wait()
    query = stacked(q_v[...], size)
    qs1_ref[...] = query
    keys = jnp.concatenate([kv0[1, 0], window(1, 0)], axis=0)
    win_ref[0] = keys
    win_ref[1] = jnp.concatenate([kv0[1, 1], window(1, 1)], axis=0)
    log_rows = log_ref[1]
    for first in range(0, heads, PAIR):
        cut = slice(first * rows, first * rows + step)
        scores = dot(keys, query[cut], NT)
        probs_ref[:, cut] = jnp.exp(scores * factor + (bias - head_rows(log_rows, first)))
    copies[1].wait()
    copies[2].wait()
    back.wait()


def others_kernel(factor, win_ref, qs_ref, g_ref, o_ref, probs_ref, near0, far0, r_ref, near_ref, far_ref, up_ref, gs_ref):
    rows, size = win_ref.shape[1] // WINDOW, win_ref.shape[2]
    values = win_ref[1]
    upstream = (g_ref[...].astype(WIDE) + r_ref[...].astype(WIDE)).astype(LOW)
    dot_rows = dots_of_rows(upstream, o_ref[...], size)
    upstream = stacked(upstream, size)
    up_ref[...] = upstream
    step = PAIR * rows
    key_sum = value_sum = 0.0
    for first in range(0, upstream.shape[0] // rows, PAIR):
        cut = slice(first * rows, first * rows + step)
        probs, grad = probs_ref[:, cut], upstream[cut]
        grad_scores = (probs * (dot(values, grad, NT) - head_rows(dot_rows, first))).astype(LOW)
        gs_ref[:, cut] = grad_scores
        key_sum += dot(grad_scores[rows:], qs_ref[cut])
        value_sum += dot(probs[rows:].astype(LOW), grad)
    key_sum = key_sum * factor
    for i, (ref, before) in enumerate(((near_ref, near0), (far_ref, far0))):
        ref[0] = before[...]
        ref[1, 0] = key_sum[i * rows : (i + 1) * rows].astype(LOW)
        ref[1, 1] = value_sum[i * rows : (i + 1) * rows].astype(LOW)


def rest_kernel(factor, win_ref, qs_ref, probs_ref, up_ref, gs_ref, _, own_ref, gq_hbm, dq_v, sem):
    rows = win_ref.shape[1] // WINDOW
    dq_v[...] = turned(dot(win_ref[0].T, gs_ref[...]) * factor, rows).astype(LOW)
    back = pltpu.make_async_copy(dq_v, gq_hbm.at[0, 1], sem)
    back.start()
    own_ref[0] = dot(gs_ref[:rows], qs_ref[...]) * factor
    own_ref[1] = dot(probs_ref[:rows].astype(LOW), up_ref[...])
    back.wait()


def sum_kernel(own0, own1, near, far, gk_ref, gv_ref):
    for micro, own in enumerate((own0, own1)):
        for which, ref in ((0, gk_ref), (1, gv_ref)):
            total = own[which] + near[micro, which].astype(WIDE) + far[micro, which].astype(WIDE)
            ref[0, micro] = total.astype(LOW)


VM = pl.BlockSpec(memory_space=pltpu.VMEM)
HB = pl.BlockSpec(memory_space=pltpu.HBM)


def shards(query_in, key_in, value_in, forward_out, log_sum, grad_out, block_order):
    rows, width = query_in.shape[2:]
    size = key_in.shape[3]
    heads = width // size
    near_rows = WINDOW * rows
    factor = 1.0 / math.sqrt(size)

    def low(*shape):
        return jax.ShapeDtypeStruct(shape, LOW)

    def wide(*shape):
        return jax.ShapeDtypeStruct(shape, WIDE)

    def call(body, name, ins, outs, in_specs=None, out_specs=None, scratch=(), share=1.0, **more):
        flops = int(2 * near_rows * heads * rows * size * share)
        return pl.pallas_call(
            body,
            in_specs=in_specs or [VM] * len(ins),
            out_specs=out_specs or [VM] * len(outs),
            out_shape=outs,
            scratch_shapes=list(scratch),
            compiler_params=pltpu.CompilerParams(vmem_limit_bytes=40 * 2**20),
            cost_estimate=pl.CostEstimate(flops=flops, bytes_accessed=1024, transcendentals=0),
            name=name,
            **more,
        )(*ins)

    dma = pltpu.SemaphoreType.DMA
    query_in, grad_out, forward_out, log_sum, block_order = (
        pltpu.with_memory_space_constraint(x, pltpu.HBM)
        for x in (query_in, grad_out, forward_out, log_sum, block_order)
    )
    kv0 = jnp.stack([key_in[0], value_in[0]], axis=1)
    upper = range(1, lax.axis_size("section"))
    kv2, kv1 = ring(kv0, 2, upper), ring(kv0, 1, upper)
    pair = (2, rows, size)

    qs, gs, rd, dqt, own0, bias, log = call(
        functools.partial(own_kernel, factor),
        "own_terms",
        (block_order, log_sum, kv0, query_in, grad_out, forward_out),
        [
            low(heads * rows, size),
            low(heads * rows, size),
            wide(8, rows),
            wide(size, heads * rows),
            wide(*pair),
            wide(near_rows, rows),
            wide(2, heads, rows),
        ],
        in_specs=[HB, HB, VM, HB, HB, HB],
        scratch=[pltpu.SMEM(block_order.shape, jnp.int32)] + [pltpu.VMEM((rows, width), LOW)] * 3 + [dma((5,))],
        share=2,
    )
    (part,) = call(
        functools.partial(query_kernel, factor),
        "query_part",
        (bias, log, kv1, kv2, qs, gs, rd, dqt),
        [low(rows, width)],
    )
    received = down(part)
    late, _ = lax.optimization_barrier((kv0, part))
    kv2_first, kv1_first = ring(late, 2, (0,)), ring(late, 1, (0,))

    grad_query, near0, far0, qs1, g1, o1, probs, win = call(
        functools.partial(middle_kernel, factor),
        "middle_terms",
        (bias, log, kv0, kv1, kv2, kv1_first, kv2_first, qs, gs, rd, dqt, query_in, grad_out, forward_out),
        [
            low(*query_in.shape),
            low(*pair),
            low(*pair),
            low(heads * rows, size),
            low(rows, width),
            low(rows, width),
            wide(near_rows, heads * rows),
            low(2, near_rows, size),
        ],
        in_specs=[VM] * 11 + [HB] * 3,
        out_specs=[HB] + [VM] * 7,
        scratch=[pltpu.VMEM((rows, width), LOW)] * 2 + [dma((4,))],
        share=0.001,
    )

    near, far, up, grad_scores = call(
        functools.partial(others_kernel, factor),
        "second_others",
        (win, qs1, g1, o1, probs, near0, far0, received),
        [low(2, *pair), low(2, *pair), low(heads * rows, size), low(near_rows, heads * rows)],
        share=2,
    )
    far, near = ring(far, -2), ring(near, -1)
    own1, grad_query = call(
        functools.partial(rest_kernel, factor),
        "second_rest",
        (win, qs1, probs, up, grad_scores, grad_query),
        [wide(*pair), low(*query_in.shape)],
        in_specs=[VM] * 5 + [HB],
        out_specs=[VM, HB],
        scratch=[pltpu.VMEM((rows, width), LOW), dma],
        input_output_aliases={5: 1},
    )
    grad_key, grad_value = call(
        sum_kernel,
        "sums",
        (own0, own1, near, far),
        [low(1, 2, rows, size)] * 2,
        share=0.01,
    )
    return (grad_query, grad_key, grad_value)


def solution(mesh):
    split = P("section", None, "ctx", None)
    return jax.shard_map(
        shards,
        mesh=mesh,
        in_specs=(split, split, split, split, P("section", None, None, "ctx"), split, P()),
        out_specs=(split, split, split),
        check_vma=False,
    )
```

```python
import functools
import math

import jax
import jax.numpy as jnp
from jax import lax
from jax.experimental import pallas as pl
from jax.experimental.pallas import tpu as pltpu
from jax.sharding import PartitionSpec as P

WINDOW = 3
PAIR = 2
NT = (((1,), (1,)), ((), ()))
NN = (((1,), (0,)), ((), ()))
LOW = jnp.bfloat16
WIDE = jnp.float32


def dot(a, b, dims=NN):
    return lax.dot_general(a, b, dims, preferred_element_type=WIDE)


def ring(value, steps):
    count = lax.axis_size("ctx")
    return lax.ppermute(value, "ctx", [(i, (i + steps) % count) for i in range(count)])


def down(value):
    count = lax.axis_size("section")
    return lax.ppermute(value, "section", [(i, i - 1) for i in range(1, count)])


def mask_bias(order_ref, rows, offsets):
    half = rows // 2
    slots = order_ref.shape[0]
    own = lax.axis_index("ctx")
    lane = lax.broadcasted_iota(jnp.int32, (half, rows), 1)
    sub = lax.broadcasted_iota(jnp.int32, (half, rows), 0)
    query = jnp.where(
        lane < half,
        order_ref[2 * own] * half + lane,
        order_ref[2 * own + 1] * half + lane - half,
    )
    blocks = []
    for offset in offsets:
        for part in range(2):
            slot = lax.rem(2 * (own - offset) + part + slots, slots)
            blocks.append(jnp.where(order_ref[slot] * half + sub <= query, 0.0, -1e30))
    return jnp.concatenate(blocks, axis=0)


def wider(bias):
    return jnp.concatenate([bias] * PAIR, axis=1)


def stacked(block, size):
    return jnp.concatenate(
        [block[:, i * size : (i + 1) * size] for i in range(block.shape[1] // size)], axis=0
    )


def head_rows(table, first):
    return jnp.concatenate([table[first + i : first + i + 1] for i in range(PAIR)], axis=1)


def dots_of_rows(upstream, out, size):
    product = upstream.astype(WIDE) * out.astype(WIDE)
    high = product.astype(LOW)
    low = (product - high.astype(WIDE)).astype(LOW)
    shape = (8, product.shape[1])
    pick = (lax.broadcasted_iota(jnp.int32, shape, 1) // size == lax.broadcasted_iota(jnp.int32, shape, 0)).astype(WIDE).astype(LOW)
    return dot(pick, high, NT) + dot(pick, low, NT)


def turned(part, rows):
    count = part.shape[1] // rows
    return jnp.concatenate([part[:, i * rows : (i + 1) * rows].T for i in range(count)], axis=1)


def joined(refs, micro, which):
    return jnp.concatenate([ref[micro, which] for ref in refs], axis=0)


def own_kernel(
    factor, order_hbm, log_hbm, kv_ref, q_hbm, g_hbm, o_hbm,
    qs_ref, gs_ref, rd_ref, dqt_ref, own_ref, bias_ref, log_ref, order_s, q_v, g_v, o_v, sems,
):
    copies = [
        pltpu.make_async_copy(source, target, sems.at[i])
        for i, (source, target) in enumerate(
            (
                (order_hbm, order_s),
                (g_hbm.at[0, 0], g_v),
                (o_hbm.at[0, 0], o_v),
                (q_hbm.at[0, 0], q_v),
                (log_hbm.at[0], log_ref),
            )
        )
    ]
    for copy in copies:
        copy.start()
    rows, size = kv_ref.shape[2], kv_ref.shape[3]
    keys, values = kv_ref[0, 0], kv_ref[0, 1]
    keys_t = keys.T
    copies[0].wait()
    bias = mask_bias(order_s, rows, range(WINDOW))
    bias_ref[...] = bias
    bias = wider(bias[:rows])
    copies[1].wait()
    copies[2].wait()
    grad = stacked(g_v[...], size)
    gs_ref[...] = grad
    dot_rows = dots_of_rows(g_v[...], o_v[...], size)
    rd_ref[...] = dot_rows
    copies[3].wait()
    query = stacked(q_v[...], size)
    qs_ref[...] = query
    copies[4].wait()
    log_rows = log_ref[0]
    step = PAIR * rows
    key_sum = value_sum = 0.0
    for first in range(0, query.shape[0] // rows, PAIR):
        cut = slice(first * rows, first * rows + step)
        probs = jnp.exp(dot(keys, query[cut], NT) * factor + (bias - head_rows(log_rows, first)))
        grad_scores = (probs * (dot(values, grad[cut], NT) - head_rows(dot_rows, first))).astype(LOW)
        dqt_ref[:, cut] = dot(keys_t, grad_scores)
        key_sum += dot(grad_scores, query[cut])
        value_sum += dot(probs.astype(LOW), grad[cut])
    own_ref[0] = key_sum * factor
    own_ref[1] = value_sum


def query_kernel(factor, bias_ref, log_ref, kv2, kv1, qs_ref, gs_ref, rd_ref, dqt_ref, dq_ref):
    rows, size = kv1.shape[2], kv1.shape[3]
    keys, values = joined((kv1, kv2), 0, 0), joined((kv1, kv2), 0, 1)
    keys_t = keys.T
    bias = wider(bias_ref[rows:])
    log_rows, dot_rows = log_ref[0], rd_ref[...]
    step = PAIR * rows
    for first in range(0, dq_ref.shape[1] // size, PAIR):
        cut = slice(first * rows, first * rows + step)
        probs = jnp.exp(dot(keys, qs_ref[cut], NT) * factor + (bias - head_rows(log_rows, first)))
        grad_scores = (probs * (dot(values, gs_ref[cut], NT) - head_rows(dot_rows, first))).astype(LOW)
        part = (dot(keys_t, grad_scores) + dqt_ref[:, cut]) * factor
        dq_ref[:, first * size : (first + PAIR) * size] = turned(part, rows).astype(LOW)


def middle_kernel(
    factor, bias_ref, log_ref, kv0, kv2, kv1, qs_ref, gs_ref, rd_ref, dq_ref, q_hbm, g_hbm, o_hbm,
    gq_hbm, near_ref, far_ref, qs1_ref, g1_ref, o1_ref, probs_ref, win_ref, q_v, sems,
):
    copies = [
        pltpu.make_async_copy(q_hbm.at[0, 1], q_v, sems.at[0]),
        pltpu.make_async_copy(g_hbm.at[0, 1], g1_ref, sems.at[1]),
        pltpu.make_async_copy(o_hbm.at[0, 1], o1_ref, sems.at[2]),
        pltpu.make_async_copy(dq_ref, gq_hbm.at[0, 0], sems.at[3]),
    ]
    for copy in copies:
        copy.start()
    rows, size = kv1.shape[2], kv1.shape[3]
    heads = qs_ref.shape[0] // rows
    keys, values = joined((kv1, kv2), 0, 0), joined((kv1, kv2), 0, 1)
    bias = wider(bias_ref[...])
    log_rows, dot_rows = log_ref[0], rd_ref[...]
    step = PAIR * rows
    key_sum = value_sum = 0.0
    for first in range(0, heads, PAIR):
        cut = slice(first * rows, first * rows + step)
        query, grad = qs_ref[cut], gs_ref[cut]
        probs = jnp.exp(dot(keys, query, NT) * factor + (bias[rows:] - head_rows(log_rows, first)))
        grad_scores = (probs * (dot(values, grad, NT) - head_rows(dot_rows, first))).astype(LOW)
        key_sum += dot(grad_scores, query)
        value_sum += dot(probs.astype(LOW), grad)
    key_sum = key_sum * factor
    for i, ref in enumerate((near_ref, far_ref)):
        ref[0] = key_sum[i * rows : (i + 1) * rows].astype(LOW)
        ref[1] = value_sum[i * rows : (i + 1) * rows].astype(LOW)
    copies[0].wait()
    query = stacked(q_v[...], size)
    qs1_ref[...] = query
    keys = joined((kv0, kv1, kv2), 1, 0)
    win_ref[0] = keys
    win_ref[1] = joined((kv0, kv1, kv2), 1, 1)
    log_rows = log_ref[1]
    for first in range(0, heads, PAIR):
        cut = slice(first * rows, first * rows + step)
        scores = dot(keys, query[cut], NT)
        probs_ref[:, cut] = jnp.exp(scores * factor + (bias - head_rows(log_rows, first)))
    for copy in copies[1:]:
        copy.wait()


def others_kernel(factor, win_ref, qs_ref, g_ref, o_ref, probs_ref, near0, far0, r_ref, near_ref, far_ref, up_ref, gs_ref):
    rows, size = win_ref.shape[1] // WINDOW, win_ref.shape[2]
    values = win_ref[1]
    upstream = (g_ref[...].astype(WIDE) + r_ref[...].astype(WIDE)).astype(LOW)
    dot_rows = dots_of_rows(upstream, o_ref[...], size)
    upstream = stacked(upstream, size)
    up_ref[...] = upstream
    step = PAIR * rows
    key_sum = value_sum = 0.0
    for first in range(0, upstream.shape[0] // rows, PAIR):
        cut = slice(first * rows, first * rows + step)
        probs, grad = probs_ref[:, cut], upstream[cut]
        grad_scores = (probs * (dot(values, grad, NT) - head_rows(dot_rows, first))).astype(LOW)
        gs_ref[:, cut] = grad_scores
        key_sum += dot(grad_scores[rows:], qs_ref[cut])
        value_sum += dot(probs[rows:].astype(LOW), grad)
    key_sum = key_sum * factor
    for i, (ref, before) in enumerate(((near_ref, near0), (far_ref, far0))):
        ref[0] = before[...]
        ref[1, 0] = key_sum[i * rows : (i + 1) * rows].astype(LOW)
        ref[1, 1] = value_sum[i * rows : (i + 1) * rows].astype(LOW)


def rest_kernel(factor, win_ref, qs_ref, probs_ref, up_ref, gs_ref, _, own_ref, gq_hbm, dq_v, sem):
    rows = win_ref.shape[1] // WINDOW
    dq_v[...] = turned(dot(win_ref[0].T, gs_ref[...]) * factor, rows).astype(LOW)
    back = pltpu.make_async_copy(dq_v, gq_hbm.at[0, 1], sem)
    back.start()
    own_ref[0] = dot(gs_ref[:rows], qs_ref[...]) * factor
    own_ref[1] = dot(probs_ref[:rows].astype(LOW), up_ref[...])
    back.wait()


def sum_kernel(own0, own1, far, near, gk_ref, gv_ref):
    for micro, own in enumerate((own0, own1)):
        for which, ref in ((0, gk_ref), (1, gv_ref)):
            total = own[which] + near[micro, which].astype(WIDE) + far[micro, which].astype(WIDE)
            ref[0, micro] = total.astype(LOW)


VM = pl.BlockSpec(memory_space=pltpu.VMEM)
HB = pl.BlockSpec(memory_space=pltpu.HBM)


def shards(query_in, key_in, value_in, forward_out, log_sum, grad_out, block_order):
    rows, width = query_in.shape[2:]
    size = key_in.shape[3]
    heads = width // size
    near_rows = WINDOW * rows
    factor = 1.0 / math.sqrt(size)

    def low(*shape):
        return jax.ShapeDtypeStruct(shape, LOW)

    def wide(*shape):
        return jax.ShapeDtypeStruct(shape, WIDE)

    def call(body, name, ins, outs, in_specs=None, out_specs=None, scratch=(), share=1.0, **more):
        flops = int(2 * near_rows * heads * rows * size * share)
        return pl.pallas_call(
            body,
            in_specs=in_specs or [VM] * len(ins),
            out_specs=out_specs or [VM] * len(outs),
            out_shape=outs,
            scratch_shapes=list(scratch),
            compiler_params=pltpu.CompilerParams(vmem_limit_bytes=40 * 2**20),
            cost_estimate=pl.CostEstimate(flops=flops, bytes_accessed=1024, transcendentals=0),
            name=name,
            **more,
        )(*ins)

    dma = pltpu.SemaphoreType.DMA
    query_in, grad_out, forward_out, log_sum, block_order = (
        pltpu.with_memory_space_constraint(x, pltpu.HBM)
        for x in (query_in, grad_out, forward_out, log_sum, block_order)
    )
    kv0 = jnp.stack([key_in[0], value_in[0]], axis=1)
    kv2, kv1 = ring(kv0, 2), ring(kv0, 1)
    pair = (2, rows, size)

    qs, gs, rd, dqt, own0, bias, log = call(
        functools.partial(own_kernel, factor),
        "own_terms",
        (block_order, log_sum, kv0, query_in, grad_out, forward_out),
        [
            low(heads * rows, size),
            low(heads * rows, size),
            wide(8, rows),
            wide(size, heads * rows),
            wide(*pair),
            wide(near_rows, rows),
            wide(2, heads, rows),
        ],
        in_specs=[HB, HB, VM, HB, HB, HB],
        scratch=[pltpu.SMEM(block_order.shape, jnp.int32)] + [pltpu.VMEM((rows, width), LOW)] * 3 + [dma((5,))],
        share=2,
    )
    (part,) = call(
        functools.partial(query_kernel, factor),
        "query_part",
        (bias, log, kv2, kv1, qs, gs, rd, dqt),
        [low(rows, width)],
    )
    received = down(part)
    grad_query, near0, far0, qs1, g1, o1, probs, win = call(
        functools.partial(middle_kernel, factor),
        "middle_terms",
        (bias, log, kv0, kv2, kv1, qs, gs, rd, part, query_in, grad_out, forward_out),
        [
            low(*query_in.shape),
            low(*pair),
            low(*pair),
            low(heads * rows, size),
            low(rows, width),
            low(rows, width),
            wide(near_rows, heads * rows),
            low(2, near_rows, size),
        ],
        in_specs=[VM] * 9 + [HB] * 3,
        out_specs=[HB] + [VM] * 7,
        scratch=[pltpu.VMEM((rows, width), LOW), dma((4,))],
        share=0.001,
    )

    near, far, up, grad_scores = call(
        functools.partial(others_kernel, factor),
        "second_others",
        (win, qs1, g1, o1, probs, near0, far0, received),
        [low(2, *pair), low(2, *pair), low(heads * rows, size), low(near_rows, heads * rows)],
        share=2,
    )
    far, near = ring(far, -2), ring(near, -1)
    own1, grad_query = call(
        functools.partial(rest_kernel, factor),
        "second_rest",
        (win, qs1, probs, up, grad_scores, grad_query),
        [wide(*pair), low(*query_in.shape)],
        in_specs=[VM] * 5 + [HB],
        out_specs=[VM, HB],
        scratch=[pltpu.VMEM((rows, width), LOW), dma],
        input_output_aliases={5: 1},
    )
    grad_key, grad_value = call(
        sum_kernel,
        "sums",
        (own0, own1, far, near),
        [low(1, 2, rows, size)] * 2,
        share=0.01,
    )
    return (grad_query, grad_key, grad_value)


def solution(mesh):
    split = P("section", None, "ctx", None)
    return jax.shard_map(
        shards,
        mesh=mesh,
        in_specs=(split, split, split, split, P("section", None, None, "ctx"), split, P()),
        out_specs=(split, split, split),
        check_vma=False,
    )
```

```python
import functools
import math

import jax
import jax.numpy as jnp
from jax import lax
from jax.experimental import pallas as pl
from jax.experimental.pallas import tpu as pltpu
from jax.sharding import PartitionSpec as P

WINDOW = 3
PAIR = 2
NT = (((1,), (1,)), ((), ()))
NN = (((1,), (0,)), ((), ()))
LOW = jnp.bfloat16
WIDE = jnp.float32


def dot(a, b, dims=NN):
    return lax.dot_general(a, b, dims, preferred_element_type=WIDE)


def ring(value, steps, sections=None):
    count = lax.axis_size("ctx")
    if sections is None:
        return lax.ppermute(value, "ctx", [(i, (i + steps) % count) for i in range(count)])
    layers = lax.axis_size("section")
    route = [(i * layers + s, (i + steps) % count * layers + s) for s in sections for i in range(count)]
    return lax.ppermute(value, ("ctx", "section"), route)


def down(value):
    count = lax.axis_size("section")
    return lax.ppermute(value, "section", [(i, i - 1) for i in range(1, count)])


def mask_bias(order_ref, rows, offsets):
    half = rows // 2
    slots = order_ref.shape[0]
    own = lax.axis_index("ctx")
    lane = lax.broadcasted_iota(jnp.int32, (half, rows), 1)
    sub = lax.broadcasted_iota(jnp.int32, (half, rows), 0)
    query = jnp.where(
        lane < half,
        order_ref[2 * own] * half + lane,
        order_ref[2 * own + 1] * half + lane - half,
    )
    blocks = []
    for offset in offsets:
        for part in range(2):
            slot = lax.rem(2 * (own - offset) + part + slots, slots)
            blocks.append(jnp.where(order_ref[slot] * half + sub <= query, 0.0, -1e30))
    return jnp.concatenate(blocks, axis=0)


def wider(bias):
    return jnp.concatenate([bias] * PAIR, axis=1)


def stacked(block, size):
    return jnp.concatenate(
        [block[:, i * size : (i + 1) * size] for i in range(block.shape[1] // size)], axis=0
    )


def head_rows(table, first):
    return jnp.concatenate([table[first + i : first + i + 1] for i in range(PAIR)], axis=1)


def dots_of_rows(upstream, out, size):
    product = upstream.astype(WIDE) * out.astype(WIDE)
    high = product.astype(LOW)
    low = (product - high.astype(WIDE)).astype(LOW)
    shape = (8, product.shape[1])
    pick = (lax.broadcasted_iota(jnp.int32, shape, 1) // size == lax.broadcasted_iota(jnp.int32, shape, 0)).astype(WIDE).astype(LOW)
    return dot(pick, high, NT) + dot(pick, low, NT)


def turned(part, rows):
    count = part.shape[1] // rows
    return jnp.concatenate([part[:, i * rows : (i + 1) * rows].T for i in range(count)], axis=1)


def joined(refs, micro, which):
    return jnp.concatenate([ref[micro, which] for ref in refs], axis=0)


def own_kernel(
    factor, order_hbm, log_hbm, kv_ref, q_hbm, g_hbm, o_hbm,
    qs_ref, gs_ref, rd_ref, dqt_ref, bias_ref, log_ref, order_s, q_v, g_v, o_v, sems,
):
    copies = [
        pltpu.make_async_copy(source, target, sems.at[i])
        for i, (source, target) in enumerate(
            (
                (order_hbm, order_s),
                (g_hbm.at[0, 0], g_v),
                (o_hbm.at[0, 0], o_v),
                (q_hbm.at[0, 0], q_v),
                (log_hbm.at[0], log_ref),
            )
        )
    ]
    for copy in copies:
        copy.start()
    rows, size = kv_ref.shape[2], kv_ref.shape[3]
    keys, values = kv_ref[0, 0], kv_ref[0, 1]
    keys_t = keys.T
    copies[0].wait()
    bias = mask_bias(order_s, rows, range(WINDOW))
    bias_ref[...] = bias
    bias = wider(bias[:rows])
    copies[1].wait()
    copies[2].wait()
    grad = stacked(g_v[...], size)
    gs_ref[...] = grad
    dot_rows = dots_of_rows(g_v[...], o_v[...], size)
    rd_ref[...] = dot_rows
    copies[3].wait()
    query = stacked(q_v[...], size)
    qs_ref[...] = query
    copies[4].wait()

    @pl.when(lax.axis_index("section") > 0)
    def _():
        log_rows = log_ref[0]
        step = PAIR * rows
        for first in range(0, query.shape[0] // rows, PAIR):
            cut = slice(first * rows, first * rows + step)
            probs = jnp.exp(dot(keys, query[cut], NT) * factor + (bias - head_rows(log_rows, first)))
            grad_scores = (probs * (dot(values, grad[cut], NT) - head_rows(dot_rows, first))).astype(LOW)
            dqt_ref[:, cut] = dot(keys_t, grad_scores)


def query_kernel(factor, bias_ref, log_ref, kv1, kv2, qs_ref, gs_ref, rd_ref, dqt_ref, dq_ref):
    @pl.when(lax.axis_index("section") > 0)
    def _():
        rows, size = kv1.shape[2], kv1.shape[3]
        keys, values = joined((kv1, kv2), 0, 0), joined((kv1, kv2), 0, 1)
        keys_t = keys.T
        bias = wider(bias_ref[rows:])
        log_rows, dot_rows = log_ref[0], rd_ref[...]
        step = PAIR * rows
        for first in range(0, dq_ref.shape[1] // size, PAIR):
            cut = slice(first * rows, first * rows + step)
            probs = jnp.exp(dot(keys, qs_ref[cut], NT) * factor + (bias - head_rows(log_rows, first)))
            grad_scores = (probs * (dot(values, gs_ref[cut], NT) - head_rows(dot_rows, first))).astype(LOW)
            part = (dot(keys_t, grad_scores) + dqt_ref[:, cut]) * factor
            dq_ref[:, first * size : (first + PAIR) * size] = turned(part, rows).astype(LOW)


def middle_kernel(
    factor, bias_ref, log_ref, kv0, kv1, kv2, kv1_first, kv2_first, qs_ref, gs_ref, rd_ref, q_hbm, g_hbm, o_hbm,
    gq_hbm, own_ref, near_ref, far_ref, qs1_ref, g1_ref, o1_ref, probs_ref, win_ref, q_v, dq_v, sems,
):
    copies = [
        pltpu.make_async_copy(q_hbm.at[0, 1], q_v, sems.at[0]),
        pltpu.make_async_copy(g_hbm.at[0, 1], g1_ref, sems.at[1]),
        pltpu.make_async_copy(o_hbm.at[0, 1], o1_ref, sems.at[2]),
    ]
    for copy in copies:
        copy.start()
    rows, size = kv1.shape[2], kv1.shape[3]
    heads = qs_ref.shape[0] // rows
    bottom = lax.axis_index("section") == 0

    def window(micro, which):
        near = jnp.where(bottom, kv1_first[micro, which], kv1[micro, which])
        far = jnp.where(bottom, kv2_first[micro, which], kv2[micro, which])
        return jnp.concatenate([kv0[micro, which], near, far], axis=0)

    keys, values = window(0, 0), window(0, 1)
    keys_t = keys.T
    bias = wider(bias_ref[...])
    log_rows, dot_rows = log_ref[0], rd_ref[...]
    step = PAIR * rows
    key_sum = value_sum = 0.0
    for first in range(0, heads, PAIR):
        cut = slice(first * rows, first * rows + step)
        query, grad = qs_ref[cut], gs_ref[cut]
        probs = jnp.exp(dot(keys, query, NT) * factor + (bias - head_rows(log_rows, first)))
        grad_scores = (probs * (dot(values, grad, NT) - head_rows(dot_rows, first))).astype(LOW)
        key_sum += dot(grad_scores, query)
        value_sum += dot(probs.astype(LOW), grad)
        part = dot(keys_t, grad_scores) * factor
        dq_v[:, first * size : (first + PAIR) * size] = turned(part, rows).astype(LOW)
    back = pltpu.make_async_copy(dq_v, gq_hbm.at[0, 0], sems.at[3])
    back.start()
    key_sum = key_sum * factor
    for i, ref in enumerate((own_ref, near_ref, far_ref)):
        ref[0] = key_sum[i * rows : (i + 1) * rows].astype(ref.dtype)
        ref[1] = value_sum[i * rows : (i + 1) * rows].astype(ref.dtype)
    copies[0].wait()
    query = stacked(q_v[...], size)
    qs1_ref[...] = query
    keys = window(1, 0)
    win_ref[0] = keys
    win_ref[1] = window(1, 1)
    log_rows = log_ref[1]
    for first in range(0, heads, PAIR):
        cut = slice(first * rows, first * rows + step)
        scores = dot(keys, query[cut], NT)
        probs_ref[:, cut] = jnp.exp(scores * factor + (bias - head_rows(log_rows, first)))
    copies[1].wait()
    copies[2].wait()
    back.wait()


def others_kernel(factor, win_ref, qs_ref, g_ref, o_ref, probs_ref, near0, far0, r_ref, near_ref, far_ref, up_ref, gs_ref):
    rows, size = win_ref.shape[1] // WINDOW, win_ref.shape[2]
    values = win_ref[1]
    upstream = (g_ref[...].astype(WIDE) + r_ref[...].astype(WIDE)).astype(LOW)
    dot_rows = dots_of_rows(upstream, o_ref[...], size)
    upstream = stacked(upstream, size)
    up_ref[...] = upstream
    step = PAIR * rows
    key_sum = value_sum = 0.0
    for first in range(0, upstream.shape[0] // rows, PAIR):
        cut = slice(first * rows, first * rows + step)
        probs, grad = probs_ref[:, cut], upstream[cut]
        grad_scores = (probs * (dot(values, grad, NT) - head_rows(dot_rows, first))).astype(LOW)
        gs_ref[:, cut] = grad_scores
        key_sum += dot(grad_scores[rows:], qs_ref[cut])
        value_sum += dot(probs[rows:].astype(LOW), grad)
    key_sum = key_sum * factor
    for i, (ref, before) in enumerate(((near_ref, near0), (far_ref, far0))):
        ref[0] = before[...]
        ref[1, 0] = key_sum[i * rows : (i + 1) * rows].astype(LOW)
        ref[1, 1] = value_sum[i * rows : (i + 1) * rows].astype(LOW)


def rest_kernel(factor, win_ref, qs_ref, probs_ref, up_ref, gs_ref, _, own_ref, gq_hbm, dq_v, sem):
    rows = win_ref.shape[1] // WINDOW
    dq_v[...] = turned(dot(win_ref[0].T, gs_ref[...]) * factor, rows).astype(LOW)
    back = pltpu.make_async_copy(dq_v, gq_hbm.at[0, 1], sem)
    back.start()
    own_ref[0] = dot(gs_ref[:rows], qs_ref[...]) * factor
    own_ref[1] = dot(probs_ref[:rows].astype(LOW), up_ref[...])
    back.wait()


def sum_kernel(own0, own1, far, near, gk_ref, gv_ref):
    for micro, own in enumerate((own0, own1)):
        for which, ref in ((0, gk_ref), (1, gv_ref)):
            total = own[which] + near[micro, which].astype(WIDE) + far[micro, which].astype(WIDE)
            ref[0, micro] = total.astype(LOW)


VM = pl.BlockSpec(memory_space=pltpu.VMEM)
HB = pl.BlockSpec(memory_space=pltpu.HBM)


def shards(query_in, key_in, value_in, forward_out, log_sum, grad_out, block_order):
    rows, width = query_in.shape[2:]
    size = key_in.shape[3]
    heads = width // size
    near_rows = WINDOW * rows
    factor = 1.0 / math.sqrt(size)

    def low(*shape):
        return jax.ShapeDtypeStruct(shape, LOW)

    def wide(*shape):
        return jax.ShapeDtypeStruct(shape, WIDE)

    def call(body, name, ins, outs, in_specs=None, out_specs=None, scratch=(), share=1.0, **more):
        flops = int(2 * near_rows * heads * rows * size * share)
        return pl.pallas_call(
            body,
            in_specs=in_specs or [VM] * len(ins),
            out_specs=out_specs or [VM] * len(outs),
            out_shape=outs,
            scratch_shapes=list(scratch),
            compiler_params=pltpu.CompilerParams(vmem_limit_bytes=40 * 2**20),
            cost_estimate=pl.CostEstimate(flops=flops, bytes_accessed=1024, transcendentals=0),
            name=name,
            **more,
        )(*ins)

    dma = pltpu.SemaphoreType.DMA
    query_in, grad_out, forward_out, log_sum, block_order = (
        pltpu.with_memory_space_constraint(x, pltpu.HBM)
        for x in (query_in, grad_out, forward_out, log_sum, block_order)
    )
    kv0 = jnp.stack([key_in[0], value_in[0]], axis=1)
    upper = range(1, lax.axis_size("section"))
    kv2, kv1 = ring(kv0, 2, upper), ring(kv0, 1, upper)
    kv2_first, kv1_first = ring(kv0, 2, (0,)), ring(kv0, 1, (0,))
    pair = (2, rows, size)

    qs, gs, rd, dqt, bias, log = call(
        functools.partial(own_kernel, factor),
        "own_terms",
        (block_order, log_sum, kv0, query_in, grad_out, forward_out),
        [
            low(heads * rows, size),
            low(heads * rows, size),
            wide(8, rows),
            wide(size, heads * rows),
            wide(near_rows, rows),
            wide(2, heads, rows),
        ],
        in_specs=[HB, HB, VM, HB, HB, HB],
        scratch=[pltpu.SMEM(block_order.shape, jnp.int32)] + [pltpu.VMEM((rows, width), LOW)] * 3 + [dma((5,))],
        share=2,
    )
    (part,) = call(
        functools.partial(query_kernel, factor),
        "query_part",
        (bias, log, kv1, kv2, qs, gs, rd, dqt),
        [low(rows, width)],
    )
    received = down(part)

    grad_query, own0, near0, far0, qs1, g1, o1, probs, win = call(
        functools.partial(middle_kernel, factor),
        "middle_terms",
        (bias, log, kv0, kv1, kv2, kv1_first, kv2_first, qs, gs, rd, query_in, grad_out, forward_out),
        [
            low(*query_in.shape),
            wide(*pair),
            low(*pair),
            low(*pair),
            low(heads * rows, size),
            low(rows, width),
            low(rows, width),
            wide(near_rows, heads * rows),
            low(2, near_rows, size),
        ],
        in_specs=[VM] * 10 + [HB] * 3,
        out_specs=[HB] + [VM] * 8,
        scratch=[pltpu.VMEM((rows, width), LOW)] * 2 + [dma((4,))],
        share=0.001,
    )

    near, far, up, grad_scores = call(
        functools.partial(others_kernel, factor),
        "second_others",
        (win, qs1, g1, o1, probs, near0, far0, received),
        [low(2, *pair), low(2, *pair), low(heads * rows, size), low(near_rows, heads * rows)],
        share=2,
    )
    far, near = ring(far, -2), ring(near, -1)
    own1, grad_query = call(
        functools.partial(rest_kernel, factor),
        "second_rest",
        (win, qs1, probs, up, grad_scores, grad_query),
        [wide(*pair), low(*query_in.shape)],
        in_specs=[VM] * 5 + [HB],
        out_specs=[VM, HB],
        scratch=[pltpu.VMEM((rows, width), LOW), dma],
        input_output_aliases={5: 1},
    )
    grad_key, grad_value = call(
        sum_kernel,
        "sums",
        (own0, own1, far, near),
        [low(1, 2, rows, size)] * 2,
        share=0.01,
    )
    return (grad_query, grad_key, grad_value)


def solution(mesh):
    split = P("section", None, "ctx", None)
    return jax.shard_map(
        shards,
        mesh=mesh,
        in_specs=(split, split, split, split, P("section", None, None, "ctx"), split, P()),
        out_specs=(split, split, split),
        check_vma=False,
    )
```

```python
import functools
import math

import jax
import jax.numpy as jnp
from jax import lax
from jax.experimental import pallas as pl
from jax.experimental.pallas import tpu as pltpu
from jax.sharding import PartitionSpec as P

WINDOW = 3
PAIR = 2
NT = (((1,), (1,)), ((), ()))
NN = (((1,), (0,)), ((), ()))
LOW = jnp.bfloat16
WIDE = jnp.float32


def dot(a, b, dims=NN):
    return lax.dot_general(a, b, dims, preferred_element_type=WIDE)


def ring(value, steps, sections=None, cores=(0, 1)):
    count = lax.axis_size("ctx")
    steps = (steps, steps) if isinstance(steps, int) else steps
    moves = [(i, (i + steps[i % 2]) % count) for i in range(count) if i % 2 in cores]
    if sections is None:
        return lax.ppermute(value, "ctx", moves)
    layers = lax.axis_size("section")
    route = [(i * layers + s, j * layers + s) for s in sections for i, j in moves]
    return lax.ppermute(value, ("ctx", "section"), route)


def down(value):
    count = lax.axis_size("section")
    return lax.ppermute(value, "section", [(i, i - 1) for i in range(1, count)])


def mask_bias(order_ref, rows, offsets):
    half = rows // 2
    slots = order_ref.shape[0]
    own = lax.axis_index("ctx")
    lane = lax.broadcasted_iota(jnp.int32, (half, rows), 1)
    sub = lax.broadcasted_iota(jnp.int32, (half, rows), 0)
    query = jnp.where(
        lane < half,
        order_ref[2 * own] * half + lane,
        order_ref[2 * own + 1] * half + lane - half,
    )
    blocks = []
    for offset in offsets:
        for part in range(2):
            slot = lax.rem(2 * (own - offset) + part + slots, slots)
            blocks.append(jnp.where(order_ref[slot] * half + sub <= query, 0.0, -1e30))
    return jnp.concatenate(blocks, axis=0)


def wider(bias):
    return jnp.concatenate([bias] * PAIR, axis=1)


def stacked(block, size):
    return jnp.concatenate(
        [block[:, i * size : (i + 1) * size] for i in range(block.shape[1] // size)], axis=0
    )


def head_rows(table, first):
    return jnp.concatenate([table[first + i : first + i + 1] for i in range(PAIR)], axis=1)


def dots_of_rows(upstream, out, size):
    product = upstream.astype(WIDE) * out.astype(WIDE)
    high = product.astype(LOW)
    low = (product - high.astype(WIDE)).astype(LOW)
    shape = (8, product.shape[1])
    pick = (lax.broadcasted_iota(jnp.int32, shape, 1) // size == lax.broadcasted_iota(jnp.int32, shape, 0)).astype(WIDE).astype(LOW)
    return dot(pick, high, NT) + dot(pick, low, NT)


def turned(part, rows):
    count = part.shape[1] // rows
    return jnp.concatenate([part[:, i * rows : (i + 1) * rows].T for i in range(count)], axis=1)


def joined(refs, micro, which):
    return jnp.concatenate([ref[micro, which] for ref in refs], axis=0)


def own_kernel(
    factor, order_hbm, log_hbm, kv_ref, q_hbm, g_hbm, o_hbm,
    qs_ref, gs_ref, rd_ref, dqt_ref, bias_ref, log_ref, order_s, q_v, g_v, o_v, sems,
):
    copies = [
        pltpu.make_async_copy(source, target, sems.at[i])
        for i, (source, target) in enumerate(
            (
                (order_hbm, order_s),
                (g_hbm.at[0, 0], g_v),
                (o_hbm.at[0, 0], o_v),
                (q_hbm.at[0, 0], q_v),
                (log_hbm.at[0], log_ref),
            )
        )
    ]
    for copy in copies:
        copy.start()
    rows, size = kv_ref.shape[2], kv_ref.shape[3]
    keys, values = kv_ref[0, 0], kv_ref[0, 1]
    keys_t = keys.T
    copies[0].wait()
    bias = mask_bias(order_s, rows, range(WINDOW))
    bias_ref[...] = bias
    bias = wider(bias[:rows])
    copies[1].wait()
    copies[2].wait()
    grad = stacked(g_v[...], size)
    gs_ref[...] = grad
    dot_rows = dots_of_rows(g_v[...], o_v[...], size)
    rd_ref[...] = dot_rows
    copies[3].wait()
    query = stacked(q_v[...], size)
    qs_ref[...] = query
    copies[4].wait()

    @pl.when(lax.axis_index("section") > 0)
    def _():
        log_rows = log_ref[0]
        step = PAIR * rows
        for first in range(0, query.shape[0] // rows, PAIR):
            cut = slice(first * rows, first * rows + step)
            probs = jnp.exp(dot(keys, query[cut], NT) * factor + (bias - head_rows(log_rows, first)))
            grad_scores = (probs * (dot(values, grad[cut], NT) - head_rows(dot_rows, first))).astype(LOW)
            dqt_ref[:, cut] = dot(keys_t, grad_scores)


def query_kernel(factor, bias_ref, log_ref, kv1, kv2, qs_ref, gs_ref, rd_ref, dqt_ref, dq_ref):
    @pl.when(lax.axis_index("section") > 0)
    def _():
        rows, size = kv1.shape[2], kv1.shape[3]
        keys, values = joined((kv1, kv2), 0, 0), joined((kv1, kv2), 0, 1)
        keys_t = keys.T
        bias = wider(bias_ref[rows:])
        log_rows, dot_rows = log_ref[0], rd_ref[...]
        step = PAIR * rows
        for first in range(0, dq_ref.shape[1] // size, PAIR):
            cut = slice(first * rows, first * rows + step)
            probs = jnp.exp(dot(keys, qs_ref[cut], NT) * factor + (bias - head_rows(log_rows, first)))
            grad_scores = (probs * (dot(values, gs_ref[cut], NT) - head_rows(dot_rows, first))).astype(LOW)
            part = (dot(keys_t, grad_scores) + dqt_ref[:, cut]) * factor
            dq_ref[:, first * size : (first + PAIR) * size] = turned(part, rows).astype(LOW)


def own_part(factor, bias_ref, log_rows, kv0, qs_ref, gs_ref, dot_rows, keys_ref, scores_ref, own_ref, dq_v):
    rows, size = kv0.shape[2], kv0.shape[3]
    keys, values = kv0[0, 0], kv0[0, 1]
    keys_t, others_t = keys.T, keys_ref[...].T
    bias = wider(bias_ref[:rows])
    step = PAIR * rows
    key_sum = value_sum = 0.0
    for first in range(0, qs_ref.shape[0] // rows, PAIR):
        cut = slice(first * rows, first * rows + step)
        query, grad = qs_ref[cut], gs_ref[cut]
        probs = jnp.exp(dot(keys, query, NT) * factor + (bias - head_rows(log_rows, first)))
        grad_scores = (probs * (dot(values, grad, NT) - head_rows(dot_rows, first))).astype(LOW)
        key_sum += dot(grad_scores, query)
        value_sum += dot(probs.astype(LOW), grad)
        part = (dot(keys_t, grad_scores) + dot(others_t, scores_ref[:, cut])) * factor
        dq_v[:, first * size : (first + PAIR) * size] = turned(part, rows).astype(LOW)
    own_ref[0] = key_sum * factor
    own_ref[1] = value_sum


def middle_kernel(
    factor, bias_ref, log_ref, kv0, kv1, kv2, inner_near, inner_far, to_odd, qs_ref, gs_ref, rd_ref, q_hbm, g_hbm, o_hbm,
    gq_hbm, own_ref, near_ref, far_ref, scores_ref, keys_ref, qs1_ref, g1_ref, o1_ref, probs_ref, win_ref, q_v, dq_v, sems,
):
    copies = [
        pltpu.make_async_copy(q_hbm.at[0, 1], q_v, sems.at[0]),
        pltpu.make_async_copy(g_hbm.at[0, 1], g1_ref, sems.at[1]),
        pltpu.make_async_copy(o_hbm.at[0, 1], o1_ref, sems.at[2]),
    ]
    for copy in copies:
        copy.start()
    rows, size = kv1.shape[2], kv1.shape[3]
    heads = qs_ref.shape[0] // rows
    bottom = lax.axis_index("section") == 0
    odd = lax.rem(lax.axis_index("ctx"), 2) == 1

    def window(micro, which):
        near = jnp.where(bottom, inner_near[micro, which], kv1[micro, which])
        far = jnp.where(odd, to_odd[micro, which], inner_far[micro, which])
        far = jnp.where(bottom, far, kv2[micro, which])
        return jnp.concatenate([near, far], axis=0)

    keys, values = window(0, 0), window(0, 1)
    keys_ref[...] = keys
    bias = wider(bias_ref[...])
    log_rows, dot_rows = log_ref[0], rd_ref[...]
    step = PAIR * rows
    key_sum = value_sum = 0.0
    for first in range(0, heads, PAIR):
        cut = slice(first * rows, first * rows + step)
        query, grad = qs_ref[cut], gs_ref[cut]
        probs = jnp.exp(dot(keys, query, NT) * factor + (bias[rows:] - head_rows(log_rows, first)))
        grad_scores = (probs * (dot(values, grad, NT) - head_rows(dot_rows, first))).astype(LOW)
        scores_ref[:, cut] = grad_scores
        key_sum += dot(grad_scores, query)
        value_sum += dot(probs.astype(LOW), grad)
    key_sum = key_sum * factor
    for i, ref in enumerate((near_ref, far_ref)):
        ref[0] = key_sum[i * rows : (i + 1) * rows].astype(LOW)
        ref[1] = value_sum[i * rows : (i + 1) * rows].astype(LOW)

    @pl.when(jnp.logical_not(bottom))
    def _():
        own_part(factor, bias_ref, log_rows, kv0, qs_ref, gs_ref, dot_rows, keys_ref, scores_ref, own_ref, dq_v)
        back = pltpu.make_async_copy(dq_v, gq_hbm.at[0, 0], sems.at[3])
        back.start()
        back.wait()

    copies[0].wait()
    query = stacked(q_v[...], size)
    qs1_ref[...] = query
    keys = jnp.concatenate([kv0[1, 0], window(1, 0)], axis=0)
    win_ref[0] = keys
    win_ref[1] = jnp.concatenate([kv0[1, 1], window(1, 1)], axis=0)
    log_rows = log_ref[1]
    for first in range(0, heads, PAIR):
        cut = slice(first * rows, first * rows + step)
        scores = dot(keys, query[cut], NT)
        probs_ref[:, cut] = jnp.exp(scores * factor + (bias - head_rows(log_rows, first)))
    copies[1].wait()
    copies[2].wait()


def others_kernel(factor, win_ref, qs_ref, g_ref, o_ref, probs_ref, near0, far0, r_ref, near_ref, far_ref, up_ref, gs_ref):
    rows, size = win_ref.shape[1] // WINDOW, win_ref.shape[2]
    values = win_ref[1]
    upstream = (g_ref[...].astype(WIDE) + r_ref[...].astype(WIDE)).astype(LOW)
    dot_rows = dots_of_rows(upstream, o_ref[...], size)
    upstream = stacked(upstream, size)
    up_ref[...] = upstream
    step = PAIR * rows
    key_sum = value_sum = 0.0
    for first in range(0, upstream.shape[0] // rows, PAIR):
        cut = slice(first * rows, first * rows + step)
        probs, grad = probs_ref[:, cut], upstream[cut]
        grad_scores = (probs * (dot(values, grad, NT) - head_rows(dot_rows, first))).astype(LOW)
        gs_ref[:, cut] = grad_scores
        key_sum += dot(grad_scores[rows:], qs_ref[cut])
        value_sum += dot(probs[rows:].astype(LOW), grad)
    key_sum = key_sum * factor
    for i, (ref, before) in enumerate(((near_ref, near0), (far_ref, far0))):
        ref[0] = before[...]
        ref[1, 0] = key_sum[i * rows : (i + 1) * rows].astype(LOW)
        ref[1, 1] = value_sum[i * rows : (i + 1) * rows].astype(LOW)


def rest_kernel(
    factor, bias_ref, log_ref, kv0, qs0_ref, gs0_ref, rd_ref, keys_ref, scores_ref, own0, win_ref, qs_ref, probs_ref, up_ref, gs_ref, _,
    own0_ref, own_ref, gq_hbm, dq0_v, dq_v, sems,
):
    rows = win_ref.shape[1] // WINDOW
    dq_v[...] = turned(dot(win_ref[0].T, gs_ref[...]) * factor, rows).astype(LOW)
    back = pltpu.make_async_copy(dq_v, gq_hbm.at[0, 1], sems.at[0])
    back.start()
    own_ref[0] = dot(gs_ref[:rows], qs_ref[...]) * factor
    own_ref[1] = dot(probs_ref[:rows].astype(LOW), up_ref[...])
    bottom = lax.axis_index("section") == 0

    @pl.when(jnp.logical_not(bottom))
    def _():
        own0_ref[...] = own0[...]

    @pl.when(bottom)
    def _():
        own_part(factor, bias_ref, log_ref[0], kv0, qs0_ref, gs0_ref, rd_ref[...], keys_ref, scores_ref, own0_ref, dq0_v)
        first = pltpu.make_async_copy(dq0_v, gq_hbm.at[0, 0], sems.at[1])
        first.start()
        first.wait()

    back.wait()


def sum_kernel(own0, own1, near, far, gk_ref, gv_ref):
    for micro, own in enumerate((own0, own1)):
        for which, ref in ((0, gk_ref), (1, gv_ref)):
            total = own[which] + near[micro, which].astype(WIDE) + far[micro, which].astype(WIDE)
            ref[0, micro] = total.astype(LOW)


VM = pl.BlockSpec(memory_space=pltpu.VMEM)
HB = pl.BlockSpec(memory_space=pltpu.HBM)


def shards(query_in, key_in, value_in, forward_out, log_sum, grad_out, block_order):
    rows, width = query_in.shape[2:]
    size = key_in.shape[3]
    heads = width // size
    near_rows = WINDOW * rows
    factor = 1.0 / math.sqrt(size)

    def low(*shape):
        return jax.ShapeDtypeStruct(shape, LOW)

    def wide(*shape):
        return jax.ShapeDtypeStruct(shape, WIDE)

    def call(body, name, ins, outs, in_specs=None, out_specs=None, scratch=(), share=1.0, **more):
        flops = int(2 * near_rows * heads * rows * size * share)
        return pl.pallas_call(
            body,
            in_specs=in_specs or [VM] * len(ins),
            out_specs=out_specs or [VM] * len(outs),
            out_shape=outs,
            scratch_shapes=list(scratch),
            compiler_params=pltpu.CompilerParams(vmem_limit_bytes=40 * 2**20),
            cost_estimate=pl.CostEstimate(flops=flops, bytes_accessed=1024, transcendentals=0),
            name=name,
            **more,
        )(*ins)

    dma = pltpu.SemaphoreType.DMA
    query_in, grad_out, forward_out, log_sum, block_order = (
        pltpu.with_memory_space_constraint(x, pltpu.HBM)
        for x in (query_in, grad_out, forward_out, log_sum, block_order)
    )
    kv0 = jnp.stack([key_in[0], value_in[0]], axis=1)
    upper = range(1, lax.axis_size("section"))
    kv2, kv1 = ring(kv0, 2, upper), ring(kv0, 1, upper)
    pair = (2, rows, size)

    qs, gs, rd, dqt, bias, log = call(
        functools.partial(own_kernel, factor),
        "own_terms",
        (block_order, log_sum, kv0, query_in, grad_out, forward_out),
        [
            low(heads * rows, size),
            low(heads * rows, size),
            wide(8, rows),
            wide(size, heads * rows),
            wide(near_rows, rows),
            wide(2, heads, rows),
        ],
        in_specs=[HB, HB, VM, HB, HB, HB],
        scratch=[pltpu.SMEM(block_order.shape, jnp.int32)] + [pltpu.VMEM((rows, width), LOW)] * 3 + [dma((5,))],
        share=2,
    )
    (part,) = call(
        functools.partial(query_kernel, factor),
        "query_part",
        (bias, log, kv1, kv2, qs, gs, rd, dqt),
        [low(rows, width)],
    )
    received = down(part)

    odd = lax.rem(lax.axis_index("ctx"), 2) == 1
    late, _ = lax.optimization_barrier((kv0, rd))
    to_odd, even_to_odd = ring(late, 2, (0,), (1,)), ring(late, 3, (0,), (0,))
    to_odd, even_to_odd, _ = lax.optimization_barrier((to_odd, even_to_odd, part))
    inner_far = ring(even_to_odd, -1, (0,), (1,))
    inner_near = ring(jnp.where(odd, to_odd, kv0), (1, -1), (0,))

    grad_query, own0, near0, far0, scores0, keys0, qs1, g1, o1, probs, win = call(
        functools.partial(middle_kernel, factor),
        "middle_terms",
        (bias, log, kv0, kv1, kv2, inner_near, inner_far, to_odd, qs, gs, rd, query_in, grad_out, forward_out),
        [
            low(*query_in.shape),
            wide(*pair),
            low(*pair),
            low(*pair),
            low((WINDOW - 1) * rows, heads * rows),
            low((WINDOW - 1) * rows, size),
            low(heads * rows, size),
            low(rows, width),
            low(rows, width),
            wide(near_rows, heads * rows),
            low(2, near_rows, size),
        ],
        in_specs=[VM] * 11 + [HB] * 3,
        out_specs=[HB] + [VM] * 10,
        scratch=[pltpu.VMEM((rows, width), LOW)] * 2 + [dma((4,))],
        share=0.001,
    )

    near, far, up, grad_scores = call(
        functools.partial(others_kernel, factor),
        "second_others",
        (win, qs1, g1, o1, probs, near0, far0, received),
        [low(2, *pair), low(2, *pair), low(heads * rows, size), low(near_rows, heads * rows)],
        share=2,
    )
    far, near = ring(far, -2), ring(near, -1)
    own0, own1, grad_query = call(
        functools.partial(rest_kernel, factor),
        "second_rest",
        (bias, log, kv0, qs, gs, rd, keys0, scores0, own0, win, qs1, probs, up, grad_scores, grad_query),
        [wide(*pair), wide(*pair), low(*query_in.shape)],
        in_specs=[VM] * 14 + [HB],
        out_specs=[VM, VM, HB],
        scratch=[pltpu.VMEM((rows, width), LOW)] * 2 + [dma((2,))],
        input_output_aliases={14: 2},
    )
    grad_key, grad_value = call(
        sum_kernel,
        "sums",
        (own0, own1, near, far),
        [low(1, 2, rows, size)] * 2,
        share=0.01,
    )
    return (grad_query, grad_key, grad_value)


def solution(mesh):
    split = P("section", None, "ctx", None)
    return jax.shard_map(
        shards,
        mesh=mesh,
        in_specs=(split, split, split, split, P("section", None, None, "ctx"), split, P()),
        out_specs=(split, split, split),
        check_vma=False,
    )
```

```python
import functools
import math

import jax
import jax.numpy as jnp
from jax import lax
from jax.experimental import pallas as pl
from jax.experimental.pallas import tpu as pltpu
from jax.sharding import PartitionSpec as P

WINDOW = 3
PAIR = 2
NT = (((1,), (1,)), ((), ()))
NN = (((1,), (0,)), ((), ()))
LOW = jnp.bfloat16
WIDE = jnp.float32


def dot(a, b, dims=NN):
    return lax.dot_general(a, b, dims, preferred_element_type=WIDE)


def ring(value, steps, sections=None, cores=(0, 1)):
    count = lax.axis_size("ctx")
    steps = (steps, steps) if isinstance(steps, int) else steps
    moves = [(i, (i + steps[i % 2]) % count) for i in range(count) if i % 2 in cores]
    if sections is None:
        return lax.ppermute(value, "ctx", moves)
    layers = lax.axis_size("section")
    route = [(i * layers + s, j * layers + s) for s in sections for i, j in moves]
    return lax.ppermute(value, ("ctx", "section"), route)


def down(value):
    count = lax.axis_size("section")
    return lax.ppermute(value, "section", [(i, i - 1) for i in range(1, count)])


def mask_bias(order_ref, rows, offsets):
    half = rows // 2
    slots = order_ref.shape[0]
    own = lax.axis_index("ctx")
    lane = lax.broadcasted_iota(jnp.int32, (half, rows), 1)
    sub = lax.broadcasted_iota(jnp.int32, (half, rows), 0)
    query = jnp.where(
        lane < half,
        order_ref[2 * own] * half + lane,
        order_ref[2 * own + 1] * half + lane - half,
    )
    blocks = []
    for offset in offsets:
        for part in range(2):
            slot = lax.rem(2 * (own - offset) + part + slots, slots)
            blocks.append(jnp.where(order_ref[slot] * half + sub <= query, 0.0, -1e30))
    return jnp.concatenate(blocks, axis=0)


def wider(bias):
    return jnp.concatenate([bias] * PAIR, axis=1)


def stacked(block, size):
    return jnp.concatenate(
        [block[:, i * size : (i + 1) * size] for i in range(block.shape[1] // size)], axis=0
    )


def head_rows(table, first):
    return jnp.concatenate([table[first + i : first + i + 1] for i in range(PAIR)], axis=1)


def dots_of_rows(upstream, out, size):
    product = upstream.astype(WIDE) * out.astype(WIDE)
    high = product.astype(LOW)
    low = (product - high.astype(WIDE)).astype(LOW)
    shape = (8, product.shape[1])
    pick = (lax.broadcasted_iota(jnp.int32, shape, 1) // size == lax.broadcasted_iota(jnp.int32, shape, 0)).astype(WIDE).astype(LOW)
    return dot(pick, high, NT) + dot(pick, low, NT)


def turned(part, rows):
    count = part.shape[1] // rows
    return jnp.concatenate([part[:, i * rows : (i + 1) * rows].T for i in range(count)], axis=1)


def joined(refs, micro, which):
    return jnp.concatenate([ref[micro, which] for ref in refs], axis=0)


def own_kernel(
    factor, order_hbm, log_hbm, kv_ref, q_hbm, g_hbm, o_hbm,
    qs_ref, gs_ref, rd_ref, dqt_ref, bias_ref, log_ref, order_s, q_v, g_v, o_v, sems,
):
    copies = [
        pltpu.make_async_copy(source, target, sems.at[i])
        for i, (source, target) in enumerate(
            (
                (order_hbm, order_s),
                (g_hbm.at[0, 0], g_v),
                (o_hbm.at[0, 0], o_v),
                (q_hbm.at[0, 0], q_v),
                (log_hbm.at[0], log_ref),
            )
        )
    ]
    for copy in copies:
        copy.start()
    rows, size = kv_ref.shape[2], kv_ref.shape[3]
    keys, values = kv_ref[0, 0], kv_ref[0, 1]
    keys_t = keys.T
    copies[0].wait()
    bias = mask_bias(order_s, rows, range(WINDOW))
    bias_ref[...] = bias
    bias = wider(bias[:rows])
    copies[1].wait()
    copies[2].wait()
    grad = stacked(g_v[...], size)
    gs_ref[...] = grad
    dot_rows = dots_of_rows(g_v[...], o_v[...], size)
    rd_ref[...] = dot_rows
    copies[3].wait()
    query = stacked(q_v[...], size)
    qs_ref[...] = query
    copies[4].wait()

    @pl.when(lax.axis_index("section") > 0)
    def _():
        log_rows = log_ref[0]
        step = PAIR * rows
        for first in range(0, query.shape[0] // rows, PAIR):
            cut = slice(first * rows, first * rows + step)
            probs = jnp.exp(dot(keys, query[cut], NT) * factor + (bias - head_rows(log_rows, first)))
            grad_scores = (probs * (dot(values, grad[cut], NT) - head_rows(dot_rows, first))).astype(LOW)
            dqt_ref[:, cut] = dot(keys_t, grad_scores)


def query_kernel(factor, bias_ref, log_ref, kv1, kv2, qs_ref, gs_ref, rd_ref, dqt_ref, dq_ref):
    @pl.when(lax.axis_index("section") > 0)
    def _():
        rows, size = kv1.shape[2], kv1.shape[3]
        keys, values = joined((kv1, kv2), 0, 0), joined((kv1, kv2), 0, 1)
        keys_t = keys.T
        bias = wider(bias_ref[rows:])
        log_rows, dot_rows = log_ref[0], rd_ref[...]
        step = PAIR * rows
        for first in range(0, dq_ref.shape[1] // size, PAIR):
            cut = slice(first * rows, first * rows + step)
            probs = jnp.exp(dot(keys, qs_ref[cut], NT) * factor + (bias - head_rows(log_rows, first)))
            grad_scores = (probs * (dot(values, gs_ref[cut], NT) - head_rows(dot_rows, first))).astype(LOW)
            part = (dot(keys_t, grad_scores) + dqt_ref[:, cut]) * factor
            dq_ref[:, first * size : (first + PAIR) * size] = turned(part, rows).astype(LOW)


def own_part(factor, bias_ref, log_rows, kv0, qs_ref, gs_ref, dot_rows, keys_ref, scores_ref, own_ref, dq_v):
    rows, size = kv0.shape[2], kv0.shape[3]
    keys, values = kv0[0, 0], kv0[0, 1]
    keys_t, others_t = keys.T, keys_ref[...].T
    bias = wider(bias_ref[:rows])
    step = PAIR * rows
    key_sum = value_sum = 0.0
    for first in range(0, qs_ref.shape[0] // rows, PAIR):
        cut = slice(first * rows, first * rows + step)
        query, grad = qs_ref[cut], gs_ref[cut]
        probs = jnp.exp(dot(keys, query, NT) * factor + (bias - head_rows(log_rows, first)))
        grad_scores = (probs * (dot(values, grad, NT) - head_rows(dot_rows, first))).astype(LOW)
        key_sum += dot(grad_scores, query)
        value_sum += dot(probs.astype(LOW), grad)
        part = (dot(keys_t, grad_scores) + dot(others_t, scores_ref[:, cut])) * factor
        dq_v[:, first * size : (first + PAIR) * size] = turned(part, rows).astype(LOW)
    own_ref[0] = key_sum * factor
    own_ref[1] = value_sum


def middle_kernel(
    factor, bias_ref, log_ref, kv0, kv1, kv2, inner_near, inner_far, to_odd, qs_ref, gs_ref, rd_ref, q_hbm, g_hbm, o_hbm,
    gq_hbm, own_ref, near_ref, far_ref, scores_ref, keys_ref, qs1_ref, g1_ref, o1_ref, probs_ref, win_ref, q_v, dq_v, sems,
):
    copies = [
        pltpu.make_async_copy(q_hbm.at[0, 1], q_v, sems.at[0]),
        pltpu.make_async_copy(g_hbm.at[0, 1], g1_ref, sems.at[1]),
        pltpu.make_async_copy(o_hbm.at[0, 1], o1_ref, sems.at[2]),
    ]
    for copy in copies:
        copy.start()
    rows, size = kv1.shape[2], kv1.shape[3]
    heads = qs_ref.shape[0] // rows
    bottom = lax.axis_index("section") == 0
    odd = lax.rem(lax.axis_index("ctx"), 2) == 1

    def window(micro, which):
        near = jnp.where(bottom, inner_near[micro, which], kv1[micro, which])
        far = jnp.where(odd, to_odd[micro, which], inner_far[micro, which])
        far = jnp.where(bottom, far, kv2[micro, which])
        return jnp.concatenate([near, far], axis=0)

    keys, values = window(0, 0), window(0, 1)
    keys_ref[...] = keys
    bias = wider(bias_ref[...])
    log_rows, dot_rows = log_ref[0], rd_ref[...]
    step = PAIR * rows
    key_sum = value_sum = 0.0
    for first in range(0, heads, PAIR):
        cut = slice(first * rows, first * rows + step)
        query, grad = qs_ref[cut], gs_ref[cut]
        probs = jnp.exp(dot(keys, query, NT) * factor + (bias[rows:] - head_rows(log_rows, first)))
        grad_scores = (probs * (dot(values, grad, NT) - head_rows(dot_rows, first))).astype(LOW)
        scores_ref[:, cut] = grad_scores
        key_sum += dot(grad_scores, query)
        value_sum += dot(probs.astype(LOW), grad)
    key_sum = key_sum * factor
    for i, ref in enumerate((near_ref, far_ref)):
        ref[0] = key_sum[i * rows : (i + 1) * rows].astype(LOW)
        ref[1] = value_sum[i * rows : (i + 1) * rows].astype(LOW)

    @pl.when(jnp.logical_not(bottom))
    def _():
        own_part(factor, bias_ref, log_rows, kv0, qs_ref, gs_ref, dot_rows, keys_ref, scores_ref, own_ref, dq_v)
        back = pltpu.make_async_copy(dq_v, gq_hbm.at[0, 0], sems.at[3])
        back.start()
        back.wait()

    copies[0].wait()
    query = stacked(q_v[...], size)
    qs1_ref[...] = query
    keys = jnp.concatenate([kv0[1, 0], window(1, 0)], axis=0)
    win_ref[0] = keys
    win_ref[1] = jnp.concatenate([kv0[1, 1], window(1, 1)], axis=0)
    log_rows = log_ref[1]
    for first in range(0, heads, PAIR):
        cut = slice(first * rows, first * rows + step)
        scores = dot(keys, query[cut], NT)
        probs_ref[:, cut] = jnp.exp(scores * factor + (bias - head_rows(log_rows, first)))
    copies[1].wait()
    copies[2].wait()


def others_kernel(factor, win_ref, qs_ref, g_ref, o_ref, probs_ref, near0, far0, r_ref, near_ref, far_ref, up_ref, gs_ref):
    rows, size = win_ref.shape[1] // WINDOW, win_ref.shape[2]
    values = win_ref[1]
    upstream = (g_ref[...].astype(WIDE) + r_ref[...].astype(WIDE)).astype(LOW)
    dot_rows = dots_of_rows(upstream, o_ref[...], size)
    upstream = stacked(upstream, size)
    up_ref[...] = upstream
    step = PAIR * rows
    key_sum = value_sum = 0.0
    for first in range(0, upstream.shape[0] // rows, PAIR):
        cut = slice(first * rows, first * rows + step)
        probs, grad = probs_ref[:, cut], upstream[cut]
        grad_scores = (probs * (dot(values, grad, NT) - head_rows(dot_rows, first))).astype(LOW)
        gs_ref[:, cut] = grad_scores
        key_sum += dot(grad_scores[rows:], qs_ref[cut])
        value_sum += dot(probs[rows:].astype(LOW), grad)
    key_sum = key_sum * factor
    for i, (ref, before) in enumerate(((near_ref, near0), (far_ref, far0))):
        ref[0] = before[...]
        ref[1, 0] = key_sum[i * rows : (i + 1) * rows].astype(LOW)
        ref[1, 1] = value_sum[i * rows : (i + 1) * rows].astype(LOW)


def rest_kernel(
    factor, bias_ref, log_ref, kv0, qs0_ref, gs0_ref, rd_ref, keys_ref, scores_ref, own0, win_ref, qs_ref, probs_ref, up_ref, gs_ref, _,
    own0_ref, own_ref, gq_hbm, dq0_v, dq_v, sems,
):
    rows = win_ref.shape[1] // WINDOW
    dq_v[...] = turned(dot(win_ref[0].T, gs_ref[...]) * factor, rows).astype(LOW)
    back = pltpu.make_async_copy(dq_v, gq_hbm.at[0, 1], sems.at[0])
    back.start()
    own_ref[0] = dot(gs_ref[:rows], qs_ref[...]) * factor
    own_ref[1] = dot(probs_ref[:rows].astype(LOW), up_ref[...])
    bottom = lax.axis_index("section") == 0

    @pl.when(jnp.logical_not(bottom))
    def _():
        own0_ref[...] = own0[...]

    @pl.when(bottom)
    def _():
        own_part(factor, bias_ref, log_ref[0], kv0, qs0_ref, gs0_ref, rd_ref[...], keys_ref, scores_ref, own0_ref, dq0_v)
        first = pltpu.make_async_copy(dq0_v, gq_hbm.at[0, 0], sems.at[1])
        first.start()
        first.wait()

    back.wait()


def sum_kernel(own0, own1, far, near, gk_ref, gv_ref):
    for micro, own in enumerate((own0, own1)):
        for which, ref in ((0, gk_ref), (1, gv_ref)):
            total = own[which] + near[micro, which].astype(WIDE) + far[micro, which].astype(WIDE)
            ref[0, micro] = total.astype(LOW)


VM = pl.BlockSpec(memory_space=pltpu.VMEM)
HB = pl.BlockSpec(memory_space=pltpu.HBM)


def shards(query_in, key_in, value_in, forward_out, log_sum, grad_out, block_order):
    rows, width = query_in.shape[2:]
    size = key_in.shape[3]
    heads = width // size
    near_rows = WINDOW * rows
    factor = 1.0 / math.sqrt(size)

    def low(*shape):
        return jax.ShapeDtypeStruct(shape, LOW)

    def wide(*shape):
        return jax.ShapeDtypeStruct(shape, WIDE)

    def call(body, name, ins, outs, in_specs=None, out_specs=None, scratch=(), share=1.0, **more):
        flops = int(2 * near_rows * heads * rows * size * share)
        return pl.pallas_call(
            body,
            in_specs=in_specs or [VM] * len(ins),
            out_specs=out_specs or [VM] * len(outs),
            out_shape=outs,
            scratch_shapes=list(scratch),
            compiler_params=pltpu.CompilerParams(vmem_limit_bytes=40 * 2**20),
            cost_estimate=pl.CostEstimate(flops=flops, bytes_accessed=1024, transcendentals=0),
            name=name,
            **more,
        )(*ins)

    dma = pltpu.SemaphoreType.DMA
    query_in, grad_out, forward_out, log_sum, block_order = (
        pltpu.with_memory_space_constraint(x, pltpu.HBM)
        for x in (query_in, grad_out, forward_out, log_sum, block_order)
    )
    kv0 = jnp.stack([key_in[0], value_in[0]], axis=1)
    upper = range(1, lax.axis_size("section"))
    kv2, kv1 = ring(kv0, 2, upper), ring(kv0, 1, upper)
    pair = (2, rows, size)

    qs, gs, rd, dqt, bias, log = call(
        functools.partial(own_kernel, factor),
        "own_terms",
        (block_order, log_sum, kv0, query_in, grad_out, forward_out),
        [
            low(heads * rows, size),
            low(heads * rows, size),
            wide(8, rows),
            wide(size, heads * rows),
            wide(near_rows, rows),
            wide(2, heads, rows),
        ],
        in_specs=[HB, HB, VM, HB, HB, HB],
        scratch=[pltpu.SMEM(block_order.shape, jnp.int32)] + [pltpu.VMEM((rows, width), LOW)] * 3 + [dma((5,))],
        share=2,
    )
    (part,) = call(
        functools.partial(query_kernel, factor),
        "query_part",
        (bias, log, kv1, kv2, qs, gs, rd, dqt),
        [low(rows, width)],
    )
    received = down(part)

    odd = lax.rem(lax.axis_index("ctx"), 2) == 1
    late, _ = lax.optimization_barrier((kv0, rd))
    to_odd, even_to_odd = ring(late, 2, (0,), (1,)), ring(late, 3, (0,), (0,))
    to_odd, even_to_odd, _ = lax.optimization_barrier((to_odd, even_to_odd, part))
    inner_far = ring(even_to_odd, -1, (0,), (1,))
    inner_near = ring(jnp.where(odd, to_odd, kv0), (1, -1), (0,))

    grad_query, own0, near0, far0, scores0, keys0, qs1, g1, o1, probs, win = call(
        functools.partial(middle_kernel, factor),
        "middle_terms",
        (bias, log, kv0, kv1, kv2, inner_near, inner_far, to_odd, qs, gs, rd, query_in, grad_out, forward_out),
        [
            low(*query_in.shape),
            wide(*pair),
            low(*pair),
            low(*pair),
            low((WINDOW - 1) * rows, heads * rows),
            low((WINDOW - 1) * rows, size),
            low(heads * rows, size),
            low(rows, width),
            low(rows, width),
            wide(near_rows, heads * rows),
            low(2, near_rows, size),
        ],
        in_specs=[VM] * 11 + [HB] * 3,
        out_specs=[HB] + [VM] * 10,
        scratch=[pltpu.VMEM((rows, width), LOW)] * 2 + [dma((4,))],
        share=0.001,
    )

    near, far, up, grad_scores = call(
        functools.partial(others_kernel, factor),
        "second_others",
        (win, qs1, g1, o1, probs, near0, far0, received),
        [low(2, *pair), low(2, *pair), low(heads * rows, size), low(near_rows, heads * rows)],
        share=2,
    )
    far, near = ring(far, -2), ring(near, -1)
    own0, own1, grad_query = call(
        functools.partial(rest_kernel, factor),
        "second_rest",
        (bias, log, kv0, qs, gs, rd, keys0, scores0, own0, win, qs1, probs, up, grad_scores, grad_query),
        [wide(*pair), wide(*pair), low(*query_in.shape)],
        in_specs=[VM] * 14 + [HB],
        out_specs=[VM, VM, HB],
        scratch=[pltpu.VMEM((rows, width), LOW)] * 2 + [dma((2,))],
        input_output_aliases={14: 2},
    )
    grad_key, grad_value = call(
        sum_kernel,
        "sums",
        (own0, own1, far, near),
        [low(1, 2, rows, size)] * 2,
        share=0.01,
    )
    return (grad_query, grad_key, grad_value)


def solution(mesh):
    split = P("section", None, "ctx", None)
    return jax.shard_map(
        shards,
        mesh=mesh,
        in_specs=(split, split, split, split, P("section", None, None, "ctx"), split, P()),
        out_specs=(split, split, split),
        check_vma=False,
    )
```

```python
import functools
import math

import jax
import jax.numpy as jnp
from jax import lax
from jax.experimental import pallas as pl
from jax.experimental.pallas import tpu as pltpu
from jax.sharding import PartitionSpec as P

WINDOW = 3
PAIR = 2
NT = (((1,), (1,)), ((), ()))
NN = (((1,), (0,)), ((), ()))
LOW = jnp.bfloat16
WIDE = jnp.float32


def dot(a, b, dims=NN):
    return lax.dot_general(a, b, dims, preferred_element_type=WIDE)


def ring(value, steps, sections=None, cores=(0, 1)):
    count = lax.axis_size("ctx")
    steps = (steps, steps) if isinstance(steps, int) else steps
    moves = [(i, (i + steps[i % 2]) % count) for i in range(count) if i % 2 in cores]
    if sections is None:
        return lax.ppermute(value, "ctx", moves)
    layers = lax.axis_size("section")
    route = [(i * layers + s, j * layers + s) for s in sections for i, j in moves]
    return lax.ppermute(value, ("ctx", "section"), route)


def down(value):
    count = lax.axis_size("section")
    return lax.ppermute(value, "section", [(i, i - 1) for i in range(1, count)])


def mask_bias(order_ref, rows, offsets):
    half = rows // 2
    slots = order_ref.shape[0]
    own = lax.axis_index("ctx")
    lane = lax.broadcasted_iota(jnp.int32, (half, rows), 1)
    sub = lax.broadcasted_iota(jnp.int32, (half, rows), 0)
    query = jnp.where(
        lane < half,
        order_ref[2 * own] * half + lane,
        order_ref[2 * own + 1] * half + lane - half,
    )
    blocks = []
    for offset in offsets:
        for part in range(2):
            slot = lax.rem(2 * (own - offset) + part + slots, slots)
            blocks.append(jnp.where(order_ref[slot] * half + sub <= query, 0.0, -1e30))
    return jnp.concatenate(blocks, axis=0)


def wider(bias):
    return jnp.concatenate([bias] * PAIR, axis=1)


def stacked(block, size):
    return jnp.concatenate(
        [block[:, i * size : (i + 1) * size] for i in range(block.shape[1] // size)], axis=0
    )


def head_rows(table, first):
    return jnp.concatenate([table[first + i : first + i + 1] for i in range(PAIR)], axis=1)


def dots_of_rows(upstream, out, size):
    product = upstream.astype(WIDE) * out.astype(WIDE)
    high = product.astype(LOW)
    low = (product - high.astype(WIDE)).astype(LOW)
    shape = (8, product.shape[1])
    pick = (lax.broadcasted_iota(jnp.int32, shape, 1) // size == lax.broadcasted_iota(jnp.int32, shape, 0)).astype(WIDE).astype(LOW)
    return dot(pick, high, NT) + dot(pick, low, NT)


def turned(part, rows):
    count = part.shape[1] // rows
    return jnp.concatenate([part[:, i * rows : (i + 1) * rows].T for i in range(count)], axis=1)


def joined(refs, micro, which):
    return jnp.concatenate([ref[micro, which] for ref in refs], axis=0)


def own_kernel(
    factor, order_hbm, log_hbm, kv_ref, q_hbm, g_hbm, o_hbm,
    qs_ref, gs_ref, rd_ref, dqt_ref, bias_ref, log_ref, order_s, q_v, g_v, o_v, sems,
):
    copies = [
        pltpu.make_async_copy(source, target, sems.at[i])
        for i, (source, target) in enumerate(
            (
                (order_hbm, order_s),
                (g_hbm.at[0, 0], g_v),
                (o_hbm.at[0, 0], o_v),
                (q_hbm.at[0, 0], q_v),
                (log_hbm.at[0], log_ref),
            )
        )
    ]
    for copy in copies:
        copy.start()
    rows, size = kv_ref.shape[2], kv_ref.shape[3]
    keys, values = kv_ref[0, 0], kv_ref[0, 1]
    keys_t = keys.T
    copies[0].wait()
    bias = mask_bias(order_s, rows, range(WINDOW))
    bias_ref[...] = bias
    bias = wider(bias[:rows])
    copies[1].wait()
    copies[2].wait()
    grad = stacked(g_v[...], size)
    gs_ref[...] = grad
    dot_rows = dots_of_rows(g_v[...], o_v[...], size)
    rd_ref[...] = dot_rows
    copies[3].wait()
    query = stacked(q_v[...], size)
    qs_ref[...] = query
    copies[4].wait()

    @pl.when(lax.axis_index("section") > 0)
    def _():
        log_rows = log_ref[0]
        step = PAIR * rows
        for first in range(0, query.shape[0] // rows, PAIR):
            cut = slice(first * rows, first * rows + step)
            probs = jnp.exp(dot(keys, query[cut], NT) * factor + (bias - head_rows(log_rows, first)))
            grad_scores = (probs * (dot(values, grad[cut], NT) - head_rows(dot_rows, first))).astype(LOW)
            dqt_ref[:, cut] = dot(keys_t, grad_scores)


def query_kernel(factor, bias_ref, log_ref, kv1, kv2, qs_ref, gs_ref, rd_ref, dqt_ref, dq_ref):
    @pl.when(lax.axis_index("section") > 0)
    def _():
        rows, size = kv1.shape[2], kv1.shape[3]
        keys, values = joined((kv1, kv2), 0, 0), joined((kv1, kv2), 0, 1)
        keys_t = keys.T
        bias = wider(bias_ref[rows:])
        log_rows, dot_rows = log_ref[0], rd_ref[...]
        step = PAIR * rows
        for first in range(0, dq_ref.shape[1] // size, PAIR):
            cut = slice(first * rows, first * rows + step)
            probs = jnp.exp(dot(keys, qs_ref[cut], NT) * factor + (bias - head_rows(log_rows, first)))
            grad_scores = (probs * (dot(values, gs_ref[cut], NT) - head_rows(dot_rows, first))).astype(LOW)
            part = (dot(keys_t, grad_scores) + dqt_ref[:, cut]) * factor
            dq_ref[:, first * size : (first + PAIR) * size] = turned(part, rows).astype(LOW)


def own_part(factor, micro, bias_ref, log_rows, kv0, qs_ref, gs_ref, dot_rows, other_keys, scores_ref, own_ref, dq_v):
    rows, size = kv0.shape[2], kv0.shape[3]
    keys, values = kv0[micro, 0], kv0[micro, 1]
    keys_t, others_t = keys.T, other_keys.T
    bias = wider(bias_ref[:rows])
    step = PAIR * rows
    key_sum = value_sum = 0.0
    for first in range(0, qs_ref.shape[0] // rows, PAIR):
        cut = slice(first * rows, first * rows + step)
        query, grad = qs_ref[cut], gs_ref[cut]
        probs = jnp.exp(dot(keys, query, NT) * factor + (bias - head_rows(log_rows, first)))
        grad_scores = (probs * (dot(values, grad, NT) - head_rows(dot_rows, first))).astype(LOW)
        key_sum += dot(grad_scores, query)
        value_sum += dot(probs.astype(LOW), grad)
        part = (dot(keys_t, grad_scores) + dot(others_t, scores_ref[:, cut])) * factor
        dq_v[:, first * size : (first + PAIR) * size] = turned(part, rows).astype(LOW)
    own_ref[0] = key_sum * factor
    own_ref[1] = value_sum


def middle_kernel(
    factor, bias_ref, log_ref, kv0, kv1, kv2, inner_near, inner_far, to_odd, qs_ref, gs_ref, rd_ref, q_hbm, g_hbm, o_hbm,
    gq_hbm, own_ref, near_ref, far_ref, scores_ref, keys_ref, qs1_ref, g1_ref, o1_ref, probs_ref, win_ref, q_v, dq_v, sems,
):
    copies = [
        pltpu.make_async_copy(q_hbm.at[0, 1], q_v, sems.at[0]),
        pltpu.make_async_copy(g_hbm.at[0, 1], g1_ref, sems.at[1]),
        pltpu.make_async_copy(o_hbm.at[0, 1], o1_ref, sems.at[2]),
    ]
    for copy in copies:
        copy.start()
    rows, size = kv1.shape[2], kv1.shape[3]
    heads = qs_ref.shape[0] // rows
    bottom = lax.axis_index("section") == 0
    odd = lax.rem(lax.axis_index("ctx"), 2) == 1

    def window(micro, which):
        near = jnp.where(bottom, inner_near[micro, which], kv1[micro, which])
        far = jnp.where(odd, to_odd[micro, which], inner_far[micro, which])
        far = jnp.where(bottom, far, kv2[micro, which])
        return jnp.concatenate([near, far], axis=0)

    keys, values = window(0, 0), window(0, 1)
    keys_ref[...] = keys
    bias = wider(bias_ref[...])
    log_rows, dot_rows = log_ref[0], rd_ref[...]
    step = PAIR * rows
    key_sum = value_sum = 0.0
    for first in range(0, heads, PAIR):
        cut = slice(first * rows, first * rows + step)
        query, grad = qs_ref[cut], gs_ref[cut]
        probs = jnp.exp(dot(keys, query, NT) * factor + (bias[rows:] - head_rows(log_rows, first)))
        grad_scores = (probs * (dot(values, grad, NT) - head_rows(dot_rows, first))).astype(LOW)
        scores_ref[:, cut] = grad_scores
        key_sum += dot(grad_scores, query)
        value_sum += dot(probs.astype(LOW), grad)
    key_sum = key_sum * factor
    for i, ref in enumerate((near_ref, far_ref)):
        ref[0] = key_sum[i * rows : (i + 1) * rows].astype(LOW)
        ref[1] = value_sum[i * rows : (i + 1) * rows].astype(LOW)

    @pl.when(jnp.logical_not(bottom))
    def _():
        own_part(factor, 0, bias_ref, log_rows, kv0, qs_ref, gs_ref, dot_rows, keys, scores_ref, own_ref, dq_v)
        back = pltpu.make_async_copy(dq_v, gq_hbm.at[0, 0], sems.at[3])
        back.start()
        back.wait()

    copies[0].wait()
    query = stacked(q_v[...], size)
    qs1_ref[...] = query
    keys = window(1, 0)
    win_ref[0] = keys
    win_ref[1] = window(1, 1)
    log_rows = log_ref[1]
    for first in range(0, heads, PAIR):
        cut = slice(first * rows, first * rows + step)
        scores = dot(keys, query[cut], NT)
        probs_ref[:, cut] = jnp.exp(scores * factor + (bias[rows:] - head_rows(log_rows, first)))
    copies[1].wait()
    copies[2].wait()


def others_kernel(factor, win_ref, qs_ref, g_ref, o_ref, probs_ref, near0, far0, r_ref, near_ref, far_ref, up_ref, rd_ref, gs_ref):
    rows, size = g_ref.shape[0], win_ref.shape[2]
    values = win_ref[1]
    upstream = (g_ref[...].astype(WIDE) + r_ref[...].astype(WIDE)).astype(LOW)
    dot_rows = dots_of_rows(upstream, o_ref[...], size)
    rd_ref[...] = dot_rows
    upstream = stacked(upstream, size)
    up_ref[...] = upstream
    step = PAIR * rows
    key_sum = value_sum = 0.0
    for first in range(0, upstream.shape[0] // rows, PAIR):
        cut = slice(first * rows, first * rows + step)
        probs, grad = probs_ref[:, cut], upstream[cut]
        grad_scores = (probs * (dot(values, grad, NT) - head_rows(dot_rows, first))).astype(LOW)
        gs_ref[:, cut] = grad_scores
        key_sum += dot(grad_scores, qs_ref[cut])
        value_sum += dot(probs.astype(LOW), grad)
    key_sum = key_sum * factor
    for i, (ref, before) in enumerate(((near_ref, near0), (far_ref, far0))):
        ref[0] = before[...]
        ref[1, 0] = key_sum[i * rows : (i + 1) * rows].astype(LOW)
        ref[1, 1] = value_sum[i * rows : (i + 1) * rows].astype(LOW)


def rest_kernel(
    factor, bias_ref, log_ref, kv0, qs0_ref, gs0_ref, rd_ref, keys_ref, scores_ref, own0, win_ref, qs_ref, up_ref, rd1_ref, gs_ref, _,
    own0_ref, own_ref, gq_hbm, dq0_v, dq_v, sems,
):
    own_part(factor, 1, bias_ref, log_ref[1], kv0, qs_ref, up_ref, rd1_ref[...], win_ref[0], gs_ref, own_ref, dq_v)
    back = pltpu.make_async_copy(dq_v, gq_hbm.at[0, 1], sems.at[0])
    back.start()
    bottom = lax.axis_index("section") == 0

    @pl.when(jnp.logical_not(bottom))
    def _():
        own0_ref[...] = own0[...]

    @pl.when(bottom)
    def _():
        own_part(factor, 0, bias_ref, log_ref[0], kv0, qs0_ref, gs0_ref, rd_ref[...], keys_ref[...], scores_ref, own0_ref, dq0_v)
        first = pltpu.make_async_copy(dq0_v, gq_hbm.at[0, 0], sems.at[1])
        first.start()
        first.wait()

    back.wait()


def sum_kernel(own0, own1, far, near, gk_ref, gv_ref):
    for micro, own in enumerate((own0, own1)):
        for which, ref in ((0, gk_ref), (1, gv_ref)):
            total = own[which] + near[micro, which].astype(WIDE) + far[micro, which].astype(WIDE)
            ref[0, micro] = total.astype(LOW)


VM = pl.BlockSpec(memory_space=pltpu.VMEM)
HB = pl.BlockSpec(memory_space=pltpu.HBM)


def shards(query_in, key_in, value_in, forward_out, log_sum, grad_out, block_order):
    rows, width = query_in.shape[2:]
    size = key_in.shape[3]
    heads = width // size
    near_rows = WINDOW * rows
    factor = 1.0 / math.sqrt(size)

    def low(*shape):
        return jax.ShapeDtypeStruct(shape, LOW)

    def wide(*shape):
        return jax.ShapeDtypeStruct(shape, WIDE)

    def call(body, name, ins, outs, in_specs=None, out_specs=None, scratch=(), share=1.0, **more):
        flops = int(2 * near_rows * heads * rows * size * share)
        return pl.pallas_call(
            body,
            in_specs=in_specs or [VM] * len(ins),
            out_specs=out_specs or [VM] * len(outs),
            out_shape=outs,
            scratch_shapes=list(scratch),
            compiler_params=pltpu.CompilerParams(vmem_limit_bytes=40 * 2**20),
            cost_estimate=pl.CostEstimate(flops=flops, bytes_accessed=1024, transcendentals=0),
            name=name,
            **more,
        )(*ins)

    dma = pltpu.SemaphoreType.DMA
    query_in, grad_out, forward_out, log_sum, block_order = (
        pltpu.with_memory_space_constraint(x, pltpu.HBM)
        for x in (query_in, grad_out, forward_out, log_sum, block_order)
    )
    kv0 = jnp.stack([key_in[0], value_in[0]], axis=1)
    upper = range(1, lax.axis_size("section"))
    kv2, kv1 = ring(kv0, 2, upper), ring(kv0, 1, upper)
    pair = (2, rows, size)

    qs, gs, rd, dqt, bias, log = call(
        functools.partial(own_kernel, factor),
        "own_terms",
        (block_order, log_sum, kv0, query_in, grad_out, forward_out),
        [
            low(heads * rows, size),
            low(heads * rows, size),
            wide(8, rows),
            wide(size, heads * rows),
            wide(near_rows, rows),
            wide(2, heads, rows),
        ],
        in_specs=[HB, HB, VM, HB, HB, HB],
        scratch=[pltpu.SMEM(block_order.shape, jnp.int32)] + [pltpu.VMEM((rows, width), LOW)] * 3 + [dma((5,))],
        share=2,
    )
    (part,) = call(
        functools.partial(query_kernel, factor),
        "query_part",
        (bias, log, kv1, kv2, qs, gs, rd, dqt),
        [low(rows, width)],
    )
    received = down(part)

    odd = lax.rem(lax.axis_index("ctx"), 2) == 1
    late, _ = lax.optimization_barrier((kv0, rd))
    to_odd, even_to_odd = ring(late, 2, (0,), (1,)), ring(late, 3, (0,), (0,))
    to_odd, even_to_odd, _ = lax.optimization_barrier((to_odd, even_to_odd, part))
    inner_far = ring(even_to_odd, -1, (0,), (1,))
    inner_near = ring(jnp.where(odd, to_odd, kv0), (1, -1), (0,))

    grad_query, own0, near0, far0, scores0, keys0, qs1, g1, o1, probs, win = call(
        functools.partial(middle_kernel, factor),
        "middle_terms",
        (bias, log, kv0, kv1, kv2, inner_near, inner_far, to_odd, qs, gs, rd, query_in, grad_out, forward_out),
        [
            low(*query_in.shape),
            wide(*pair),
            low(*pair),
            low(*pair),
            low((WINDOW - 1) * rows, heads * rows),
            low((WINDOW - 1) * rows, size),
            low(heads * rows, size),
            low(rows, width),
            low(rows, width),
            wide((WINDOW - 1) * rows, heads * rows),
            low(2, (WINDOW - 1) * rows, size),
        ],
        in_specs=[VM] * 11 + [HB] * 3,
        out_specs=[HB] + [VM] * 10,
        scratch=[pltpu.VMEM((rows, width), LOW)] * 2 + [dma((4,))],
        share=0.001,
    )

    near, far, up, rd1, grad_scores = call(
        functools.partial(others_kernel, factor),
        "second_others",
        (win, qs1, g1, o1, probs, near0, far0, received),
        [low(2, *pair), low(2, *pair), low(heads * rows, size), wide(8, rows), low((WINDOW - 1) * rows, heads * rows)],
        share=2,
    )
    far, near = ring(far, -2), ring(near, -1)
    own0, own1, grad_query = call(
        functools.partial(rest_kernel, factor),
        "second_rest",
        (bias, log, kv0, qs, gs, rd, keys0, scores0, own0, win, qs1, up, rd1, grad_scores, grad_query),
        [wide(*pair), wide(*pair), low(*query_in.shape)],
        in_specs=[VM] * 14 + [HB],
        out_specs=[VM, VM, HB],
        scratch=[pltpu.VMEM((rows, width), LOW)] * 2 + [dma((2,))],
        input_output_aliases={14: 2},
    )
    grad_key, grad_value = call(
        sum_kernel,
        "sums",
        (own0, own1, far, near),
        [low(1, 2, rows, size)] * 2,
        share=0.01,
    )
    return (grad_query, grad_key, grad_value)


def solution(mesh):
    split = P("section", None, "ctx", None)
    return jax.shard_map(
        shards,
        mesh=mesh,
        in_specs=(split, split, split, split, P("section", None, None, "ctx"), split, P()),
        out_specs=(split, split, split),
        check_vma=False,
    )
```
